512 devices in a mesh: row: 64 (over z, y), col: 8 (over x, core).
Axes of the slice: x: 4, y: 4, z: 16, core: 2. Of those that a mesh axis runs over, the one named last changes fastest.
Arguments:
- block_vals: bfloat16 [128, 1024, 128], P('row', 'col'), may hold values from -6 to 6
- block_slot: int32 [128, 8], P('row', 'col'), may hold values from 0 to 191, as said below
- block_count: int32 [64, 8], P('row', 'col'), may hold values from 1 to 2, as said below
- omega: bfloat16 [24576, 256], P('col'), may hold values from -6 to 6
Outputs:
- basis: bfloat16 [65536, 256], P(('row', 'col'))
- projected: float32 [8, 3072, 256], P('col', 'row')
- core: float32 [256, 256], replicated
The draws below stay inside these ranges and needn't reach their ends.
Inputs may be any that keep to these rules, and one draw needn't show every extreme that they name: `block_slot`: within one device's 2 slots each block position appears at most once; position s is row block s // 24 and column block s % 24 of that device's shard. `block_count`: some device has all 2 slots live in every draw.
All inputs are finite; a program needn't handle non-finite values.
Results may differ from the reference program's by a relative error of at most 0.0015.
The reference program's roundings to bfloat16 on the way count: a program that leaves them out, or rounds other values in their place, can miss the bound.
Values may be sent and summed in bfloat16 or wider, within the bound.
A program may use at most 64 MiB of HBM per device.

```python
import jax
import jax.numpy as jnp
from jax import lax

BS = 128
L = 256
RB = 8
CB = 24
NBD = 2
M = 65536
N = 24576
N_ROW = 64
N_COL = 8


def device_slots(key):
    first, second = jax.random.split(key)
    perm = jax.random.permutation(first, RB * CB).astype(jnp.int32)
    where_top = jnp.argmax((perm == RB * CB - 1).astype(jnp.int32)).astype(jnp.int32)
    target = jax.random.randint(second, (), 0, NBD).astype(jnp.int32)
    moved = perm[target]
    perm = perm.at[where_top].set(moved)
    perm = perm.at[target].set(RB * CB - 1)
    return perm[:NBD]


def draw_block_slot(key, part):
    key = jax.random.fold_in(key, 1)
    keys = jax.random.split(key, N_ROW * N_COL)
    perms = jax.vmap(device_slots)(keys)
    return perms.reshape(N_ROW, N_COL, NBD).transpose(0, 2, 1).reshape(N_ROW * NBD, N_COL).astype(jnp.int32)


def draw_block_count(key, part):
    key = jax.random.fold_in(key, 2)
    first, second = jax.random.split(key)
    counts = jax.random.randint(first, (N_ROW * N_COL,), max(1, NBD // 4), NBD + 1)
    chosen = jax.random.randint(second, (), 0, N_ROW * N_COL)
    counts = counts.at[chosen].set(NBD)
    return counts.reshape(N_ROW, N_COL).astype(jnp.int32)


def block_scale(key, extent, cuts, low, top_value):
    loudness, own = 1.0, jax.random.fold_in(key, 6)
    for dim, parts in cuts:
        draws = jnp.exp(jax.random.uniform(jax.random.fold_in(own, dim), (parts,), jnp.float32, low / len(cuts), top_value / len(cuts)))
        loudness = loudness * jnp.repeat(draws, extent[dim] // parts).reshape([-1 if axis == dim else 1 for axis in range(len(extent))])
    return loudness


def noise(stream_key, dims, deviation, limit, cuts=(), held_as=jnp.bfloat16):
    values = jax.random.normal(stream_key, dims, jnp.float32) * deviation
    if len(cuts) > 0:
        values = block_scale(stream_key, dims, cuts, -0.22, 0.18) * values
    return jnp.clip(values, min=-limit, max=limit).astype(held_as)


def setup_inputs(seed: int = 0) -> dict:
    arg_keys = jax.random.split(jax.random.key(seed), 5)
    block_vals = noise(arg_keys[0], (N_ROW * NBD, N_COL * BS, BS), 1.0, 6.0, ((0, 64), (1, 8)))
    block_slot = draw_block_slot(jax.random.fold_in(arg_keys[4], 71), 0)
    block_count = draw_block_count(jax.random.fold_in(arg_keys[4], 71), 0)
    omega = noise(arg_keys[3], (N, L), 1.0, 6.0, ((0, 8),))
    return {"block_vals": block_vals, "block_slot": block_slot, "block_count": block_count, "omega": omega}


def reference(block_vals, block_slot, block_count, omega):
    values = block_vals.reshape(N_ROW, NBD, N_COL, BS, BS).transpose(0, 2, 1, 3, 4)
    slots = block_slot.reshape(N_ROW, NBD, N_COL).transpose(0, 2, 1)
    omega_blocks = omega.reshape(N_COL, CB, BS, L)
    live = jnp.arange(NBD)[None, None, :] < block_count[:, :, None]

    def sketch_rows(items):
        vals_r, slot_r, live_r = items
        row_blk = slot_r // CB
        col_blk = slot_r % CB
        picked = omega_blocks[jnp.arange(N_COL)[:, None], col_blk]
        prod = jnp.einsum('cbij,cbjl->cbil', vals_r.astype(jnp.float32), picked.astype(jnp.float32))
        select = ((row_blk[..., None] == jnp.arange(RB)[None, None, :]) & live_r[..., None]).astype(jnp.float32)
        return jnp.einsum('cbr,cbil->ril', select, prod, precision=lax.Precision.HIGHEST)
    sketch = lax.map(sketch_rows, (values, slots, live)).reshape(M, L)
    gram = jnp.dot(sketch.T.astype(jnp.float32), sketch.astype(jnp.float32), precision=lax.Precision.HIGHEST, preferred_element_type=jnp.float32) / M
    chol = jnp.linalg.cholesky(gram)
    inverse = jax.scipy.linalg.solve_triangular(chol, jnp.eye(L, dtype=jnp.float32), lower=True)
    basis = jnp.dot(sketch.astype(jnp.float32), inverse.T.astype(jnp.float32), precision=lax.Precision.HIGHEST, preferred_element_type=jnp.float32).astype(jnp.bfloat16)
    basis_blocks = basis.reshape(N_ROW, RB, BS, L)

    def add_columns(total, items):
        vals_r, slot_r, live_r, basis_r = items
        row_blk = slot_r // CB
        col_blk = slot_r % CB
        picked = basis_r[row_blk]
        prod = jnp.einsum('cbji,cbjl->cbil', vals_r.astype(jnp.float32), picked.astype(jnp.float32))
        select = ((col_blk[..., None] == jnp.arange(CB)[None, None, :]) & live_r[..., None]).astype(jnp.float32)
        return (total + jnp.einsum('cbk,cbil->ckil', select, prod, precision=lax.Precision.HIGHEST), None)
    start = jnp.zeros((N_COL, CB, BS, L), jnp.float32)
    summed, unused = lax.scan(add_columns, start, (values, slots, live, basis_blocks))
    projected = summed.reshape(N_COL, CB * BS, L) / jnp.sqrt(jnp.float32(M))
    core = jnp.einsum('cil,cim->lm', projected, projected, precision=lax.Precision.HIGHEST) / N
    return (basis, projected, core)
```

```python
import functools

import jax
import jax.numpy as jnp
from jax import lax
from jax.experimental import pallas as pl
from jax.experimental.pallas import tpu as pltpu
from jax.sharding import PartitionSpec as P

MESH = pl.DeviceIdType.MESH
HI = lax.Precision.HIGHEST
F32 = jnp.float32

RB = 8
BS = 128
RANK = 256
NY, NZ, NX, NK = 4, 16, 4, 2
NQ = NY * NX * NK
PIECE = RANK // NQ
STRIP = 48
PB = 32
FAR = (6, -6, 2, -2)


def inverse_factor(a_ref, out_ref):
    n = a_ref.shape[0]
    lane = lax.broadcasted_iota(jnp.int32, (PB, n), 1)
    sub = lax.broadcasted_iota(jnp.int32, (PB, n), 0)
    sub8 = lax.broadcasted_iota(jnp.int32, (8, 128), 0)
    lane_rest = lax.broadcasted_iota(jnp.int32, (n - PB, n), 1)
    tiles, halves = PB // 8, n // 128

    def panel(p, carry):
        top = a_ref[0:PB, :]
        cols = []
        for j in range(PB):
            wide = jnp.broadcast_to(top[:, j : j + 1], (PB, 128))
            cols.append([wide[8 * t : 8 * t + 8] for t in range(tiles)])
        strip = jnp.where(lane < PB, (lane == sub).astype(F32), top)
        w = [
            [strip[8 * t : 8 * t + 8, 128 * h : 128 * h + 128] for h in range(halves)]
            for t in range(tiles)
        ]
        for k in range(PB):
            tk, sk = divmod(k, 8)
            r = lax.rsqrt(jnp.broadcast_to(cols[k][tk][sk : sk + 1], (8, 128)))
            m = [cols[k][t] * r if t >= tk else None for t in range(tiles)]
            m[tk] = jnp.where(sub8 > sk, m[tk], 0.0)
            for j in range(k + 1, PB):
                c = jnp.broadcast_to(cols[j][tk][sk : sk + 1], (8, 128)) * r
                for t in range(tk, tiles):
                    cols[j][t] = cols[j][t] - m[t] * c
            for h in range(halves):
                u = jnp.broadcast_to(w[tk][h][sk : sk + 1], (8, 128)) * r
                for t in range(tk, tiles):
                    w[t][h] = w[t][h] - m[t] * u
                w[tk][h] = jnp.where(sub8 == sk, u, w[tk][h])
        done = jnp.concatenate([jnp.concatenate(row, axis=1) for row in w], axis=0)
        placed = pltpu.roll(done, p * PB, 1)
        out_ref[pl.ds(pl.multiple_of(p * PB, PB), PB), :] = jnp.where(
            lane < (p + 1) * PB, placed, 0.0
        )
        turned = pltpu.roll(done, n - PB, 1)
        rest = pltpu.roll(jnp.where(lane_rest < PB, 0.0, a_ref[PB:n, :]), n - PB, 1)
        step = lax.dot_general(
            turned, turned, (((0,), (0,)), ((), ())), precision=HI, preferred_element_type=F32
        )
        a_ref[0 : n - PB, :] = rest - step[0 : n - PB]
        return carry

    lax.fori_loop(0, n // PB, panel, 0)


def kernel(
    vals_ref, slot_ref, count_ref, omega_ref,
    basis_ref, proj_ref, core_ref,
    part, r1, r2, own, s_all, pick, a_all, meta,
    g_send, g_recv, z_send, z_recv, g_all,
    gram, linv, prod, strip, w1, w2s, w2r,
    send_sem, r1_sem, r2_sem, s_sem, sib_sem, a_sem, m_sem, pick_sem,
    g_sem, z_sem, ag_sem, w1_sem, w2_sem,
):
    row, col = lax.axis_index("row"), lax.axis_index("col")
    z, y = row // NY, row % NY
    x, k = col // NK, col % NK
    sib = 1 - k
    q = y * (NX * NK) + col

    def at(zz, yy, xx, kk):
        return (zz * NY + yy, xx * NK + kk)

    def plane(qq):
        return (z * NY + qq // (NX * NK), qq % (NX * NK))

    def copy(src, dst, recv_sem, device):
        return pltpu.make_async_remote_copy(
            src_ref=src, dst_ref=dst, send_sem=send_sem, recv_sem=recv_sem,
            device_id=device, device_id_type=MESH,
        )

    def loop(lo, hi, f):
        def step(i, carry):
            f(i)
            return carry

        lax.fori_loop(lo, hi, step, 0)

    barrier = pltpu.get_barrier_semaphore()

    def greet_plane(j):
        pl.semaphore_signal(
            barrier, inc=1, device_id=plane((q + j) % NQ), device_id_type=MESH
        )

    def greet_ring(j):
        pl.semaphore_signal(
            barrier, inc=1, device_id=at((z + j) % NZ, y, x, k), device_id_type=MESH
        )

    loop(1, NZ, greet_ring)
    loop(1, NQ, greet_plane)

    col_blocks = omega_ref.shape[0]
    slots = vals_ref.shape[0]
    row_of, live, prods = [], [], []
    for b in range(slots):
        slot = slot_ref[b, 0]
        on = count_ref[0, 0] > b
        row_of.append(slot // col_blocks)
        live.append(jnp.where(on, 1.0, 0.0).astype(F32))
        picked = omega_ref[pl.ds(slot % col_blocks, 1)].reshape(BS, RANK)
        prods.append(jnp.dot(vals_ref[b], picked, preferred_element_type=F32))
        a_all[pl.ds(y, 1), b] = (vals_ref[b] * live[b].astype(jnp.bfloat16))[None]
        meta[pl.ds(y, 1), b] = jnp.full(
            (1,) + meta.shape[2:], jnp.where(on, slot % col_blocks, -1), jnp.int32
        )

    def fill(kk):
        for xx in range(NX):
            block = xx * NK + kk
            total = None
            for b in range(slots):
                term = prods[b] * (jnp.where(row_of[b] == block, 1.0, 0.0).astype(F32) * live[b])
                total = term if total is None else total + term
            part[pl.ds(kk, 1), xx] = total[None]

    fill(sib)
    pl.semaphore_wait(barrier, NQ - 1 + NZ - 1)

    to_sib = at(z, y, x, sib)

    def sib_copy(xx):
        return copy(part.at[sib, xx], r1.at[xx], r1_sem.at[xx], to_sib)

    def x_copy(d):
        xx = (x + d) % NX
        return copy(part.at[k, xx], r2.at[d - 1], r2_sem.at[d - 1], at(z, y, xx, k))

    order = (2, 1, 3, 0)
    for d in order:
        sib_copy((x + d) % NX).start()
    fill(k)
    for d in order:
        xx = (x + d) % NX
        sib_copy(xx).wait_recv()
        part[pl.ds(k, 1), pl.ds(xx, 1)] = (
            part[pl.ds(k, 1), pl.ds(xx, 1)] + r1[pl.ds(xx, 1)][None]
        )
        if d:
            x_copy(d).start()

    def a_copies(d):
        to = at(z, (y + d) % NY, x, k)
        return (
            copy(a_all.at[y], a_all.at[y], a_sem.at[d - 1], to),
            copy(meta.at[y], meta.at[y], m_sem.at[d - 1], to),
        )

    for d in (2, 1, 3):
        for c in a_copies(d):
            c.start()
    for d in (1, 3, 2):
        x_copy(d).wait_recv()
    own[...] = (
        part[pl.ds(k, 1), pl.ds(x, 1)].reshape(BS, RANK) + r2[0] + r2[1] + r2[2]
    )

    def gram_of(rows):
        return lax.dot_general(
            rows, rows, (((0,), (0,)), ((), ())), precision=HI, preferred_element_type=F32
        )

    def reduce_start(u, term):
        g_send[u] = term.reshape(NQ, PIECE, RANK)

        def send(j):
            qq = (q + j) % NQ
            copy(g_send.at[u, qq], g_recv.at[u, q], g_sem.at[u, q], plane(qq)).start()

        loop(1, NQ, send)
        g_recv[u, pl.ds(q, 1)] = g_send[u, pl.ds(q, 1)]

    def reduce_plane(u):
        def arrive(j):
            qq = (q + j) % NQ
            copy(g_send.at[u, q], g_recv.at[u, qq], g_sem.at[u, qq], plane(qq)).wait_recv()

        loop(1, NQ, arrive)
        total = g_recv[u, 0]
        for i in range(1, NQ):
            total = total + g_recv[u, i]
        z_send[u] = total
        z_recv[u, pl.ds(z, 1)] = total[None]

        def send(j):
            copy(
                z_send.at[u], z_recv.at[u, z], z_sem.at[u, z], at((z + j) % NZ, y, x, k)
            ).start()

        for j in (8, 7, 9, 6, 10, 5, 11, 4, 12, 3, 13, 2, 14, 1, 15):
            send(j)

    def reduce_ring(u):
        def arrive(j):
            zz = (z + j) % NZ
            copy(z_send.at[u], z_recv.at[u, zz], z_sem.at[u, zz], at(zz, y, x, k)).wait_recv()

        loop(1, NZ, arrive)
        total = z_recv[u, 0]
        for i in range(1, NZ):
            total = total + z_recv[u, i]
        g_all[u, pl.ds(q, 1)] = total[None]

        def send(j):
            copy(g_all.at[u, q], g_all.at[u, q], ag_sem.at[u, q], plane((q + j) % NQ)).start()

        loop(1, NQ, send)

    def gather_plane(u):
        def arrive(j):
            qq = (q + j) % NQ
            copy(g_all.at[u, q], g_all.at[u, qq], ag_sem.at[u, qq], plane(qq)).wait_recv()

        loop(1, NQ, arrive)
        return g_all[u].reshape(RANK, RANK)

    reduce_start(0, gram_of(own[...]))
    reduce_plane(0)

    def s_copy(d):
        return copy(own, s_all.at[k, x], s_sem.at[d - 1], at(z, y, (x + d) % NX, k))

    def s_arrival(d):
        return copy(own, s_all.at[k, (x + NX - d) % NX], s_sem.at[d - 1], to_sib)

    s_all[pl.ds(k, 1), pl.ds(x, 1)] = own[...][None, None]
    for d in (2, 1, 3):
        s_copy(d).start()
    reduce_ring(0)
    for d in (1, 3, 2):
        s_arrival(d).wait_recv()
    s_sib = copy(s_all.at[k], s_all.at[k], sib_sem, to_sib)
    s_sib.start()
    copy(s_all.at[k], s_all.at[sib], sib_sem, to_sib).wait_recv()
    for b in range(slots):
        rows = s_all[pl.ds(row_of[b] % NK, 1), pl.ds(row_of[b] // NK, 1)]
        pick[pl.ds(y, 1), b] = rows.reshape(1, BS, RANK)
    gram[...] = gather_plane(0) * (1.0 / (BS * RB * NY * NZ))

    def pick_copy(d):
        return copy(pick.at[y], pick.at[y], pick_sem.at[d - 1], at(z, (y + d) % NY, x, k))

    def pick_arrival(d):
        yy = (y + NY - d) % NY
        return copy(pick.at[y], pick.at[yy], pick_sem.at[d - 1], at(z, yy, x, k))

    for d in (2, 1, 3):
        pick_copy(d).start()
    inverse_factor(gram, linv)

    def basis_rows(rows):
        return lax.dot_general(
            rows, linv[...], (((1,), (1,)), ((), ())), precision=HI, preferred_element_type=F32
        ).astype(jnp.bfloat16)

    basis_ref[...] = basis_rows(own[...])

    def products(yy):
        for b in range(slots):
            rows = basis_rows(pick[pl.ds(yy, 1), b].reshape(BS, RANK))
            block = a_all[pl.ds(yy, 1), b].reshape(BS, BS)
            prod[pl.ds(yy, 1), b] = lax.dot_general(
                block, rows, (((0,), (0,)), ((), ())), preferred_element_type=F32
            )[None]

    products(y)
    for d in (1, 3, 2):
        yy = (y + NY - d) % NY
        to = at(z, yy, x, k)
        copy(a_all.at[y], a_all.at[yy], a_sem.at[d - 1], to).wait_recv()
        copy(meta.at[y], meta.at[yy], m_sem.at[d - 1], to).wait_recv()
        pick_arrival(d).wait_recv()
        products(yy)

    tile = 16
    per_strip = STRIP // tile

    def place(zz):
        for t in range(per_strip):
            g = zz * (NY * per_strip) + y * per_strip + t
            block, rows = g // (BS // tile), pl.multiple_of(g % (BS // tile) * tile, tile)
            total = jnp.zeros((tile, RANK), F32)
            for yy in range(NY):
                for b in range(slots):
                    total = total + jnp.where(
                        meta[yy, b] == block, prod[yy, b, pl.ds(rows, tile), :], 0.0
                    )
            strip[pl.ds(zz, 1), pl.ds(t * tile, tile), :] = total[None]

    loop(0, NZ, place)

    sign = 1 - 2 * k
    near = (1, -1, 2)

    def w1_copy(i, e):
        mid = (z + sign * near[i] + NZ) % NZ
        dest = (mid + FAR[e] + NZ) % NZ
        return copy(strip.at[dest], w1.at[e, i], w1_sem.at[e, i], at(mid, y, x, k))

    def w2_copy(e):
        return copy(w2s.at[e], w2r.at[e], w2_sem.at[e], at((z + FAR[e] + NZ) % NZ, y, x, k))

    for e in range(4):
        for i in (2, 0, 1):
            w1_copy(i, e).start()
    for e in range(4):
        for i in range(3):
            w1_copy(i, e).wait_recv()
        dest = (z + FAR[e] + NZ) % NZ
        mine = strip[pl.ds(dest, 1)].reshape(STRIP, RANK)
        w2s[e] = mine + w1[e, 0] + w1[e, 1] + w1[e, 2]
        w2_copy(e).start()
    for e in (2, 3, 0, 1):
        w2_copy(e).wait_recv()
    proj = (w2r[0] + w2r[1] + w2r[2] + w2r[3]) * (1.0 / 256.0)
    proj_ref[0] = proj

    reduce_start(1, gram_of(proj))
    reduce_plane(1)
    reduce_ring(1)
    core_ref[...] = gather_plane(1) / float(col_blocks * BS * NX * NK)

    for xx in range(NX):
        sib_copy(xx).wait_send()
    for d in (1, 2, 3):
        x_copy(d).wait_send()
        s_copy(d).wait_send()
        pick_copy(d).wait_send()
        for c in a_copies(d):
            c.wait_send()
    s_sib.wait_send()
    for u in range(2):

        def sent_plane(j):
            copy(g_send.at[u, q], g_recv.at[u, q], g_sem.at[u, q], to_sib).wait_send()
            copy(g_all.at[u, q], g_all.at[u, q], ag_sem.at[u, q], to_sib).wait_send()

        def sent_ring(j):
            copy(z_send.at[u], z_recv.at[u, z], z_sem.at[u, z], to_sib).wait_send()

        loop(1, NQ, sent_plane)
        loop(1, NZ, sent_ring)
    for e in range(4):
        for i in range(3):
            w1_copy(i, e).wait_send()
        w2_copy(e).wait_send()


def body(block_vals, block_slot, block_count, omega):
    slots = block_vals.shape[0]
    vmem, smem = pl.BlockSpec(memory_space=pltpu.VMEM), pl.BlockSpec(memory_space=pltpu.SMEM)
    dma = pltpu.SemaphoreType.DMA
    blocks = lambda *lead: pltpu.VMEM((*lead, BS, RANK), F32)
    basis, projected, core = pl.pallas_call(
        kernel,
        out_shape=(
            jax.ShapeDtypeStruct((BS, RANK), jnp.bfloat16),
            jax.ShapeDtypeStruct((1, STRIP, RANK), F32),
            jax.ShapeDtypeStruct((RANK, RANK), F32),
        ),
        in_specs=[vmem, smem, smem, vmem],
        out_specs=(vmem, vmem, vmem),
        scratch_shapes=[
            blocks(NK, NX),
            blocks(NX),
            blocks(NX - 1),
            blocks(),
            blocks(NK, NX),
            blocks(NY, slots),
            pltpu.VMEM((NY, slots, BS, BS), jnp.bfloat16),
            pltpu.VMEM((NY, slots, 16, RANK), jnp.int32),
            pltpu.VMEM((2, NQ, PIECE, RANK), F32),
            pltpu.VMEM((2, NQ, PIECE, RANK), F32),
            pltpu.VMEM((2, PIECE, RANK), F32),
            pltpu.VMEM((2, NZ, PIECE, RANK), F32),
            pltpu.VMEM((2, NQ, PIECE, RANK), F32),
            pltpu.VMEM((RANK, RANK), F32),
            pltpu.VMEM((RANK, RANK), F32),
            blocks(NY, slots),
            pltpu.VMEM((NZ, STRIP, RANK), F32),
            pltpu.VMEM((4, 3, STRIP, RANK), F32),
            pltpu.VMEM((4, STRIP, RANK), F32),
            pltpu.VMEM((4, STRIP, RANK), F32),
            dma,
            dma((NX,)), dma((NX - 1,)), dma((NX - 1,)), dma, dma((NY - 1,)), dma((NY - 1,)), dma((NY - 1,)),
            dma((2, NQ)), dma((2, NZ)), dma((2, NQ)), dma((4, 3)), dma((4,)),
        ],
        compiler_params=pltpu.CompilerParams(
            collective_id=0, has_side_effects=True, vmem_limit_bytes=48 * 2**20
        ),
        name="range_basis",
    )(block_vals, block_slot, block_count, omega.reshape(-1, BS, RANK))
    return basis, projected, core


def solution(mesh):
    placed = (P("row", "col", None), P("row", "col"), P("row", "col"), P("col", None))
    return jax.shard_map(
        body,
        mesh=mesh,
        in_specs=placed,
        out_specs=(P(("row", "col"), None), P("col", "row", None), P()),
        check_vma=False,
    )
```

```python
import functools

import jax
import jax.numpy as jnp
from jax import lax
from jax.experimental import pallas as pl
from jax.experimental.pallas import tpu as pltpu
from jax.sharding import PartitionSpec as P

MESH = pl.DeviceIdType.MESH
HI = lax.Precision.HIGHEST
F32 = jnp.float32

RB = 8
BS = 128
RANK = 256
NY, NZ, NX, NK = 4, 16, 4, 2
NQ = NY * NX
HALF = RANK // NK
PIECE = HALF // NQ
STRIP = 48
PB, SB = 64, 16
NG = 4
STEPS = 32767.0
FAR = (6, -6, 2, -2)


def inverse_factor(a_ref, out_ref):
    n = a_ref.shape[0]
    lane = lax.broadcasted_iota(jnp.int32, (PB, n), 1)
    lane8 = lax.broadcasted_iota(jnp.int32, (8, 128), 1)
    sub8 = lax.broadcasted_iota(jnp.int32, (8, 128), 0)
    lane_rest = lax.broadcasted_iota(jnp.int32, (n - PB, n), 1)
    tiles, halves = PB // 8, n // 128

    def wide(v, i):
        return jnp.broadcast_to(v[i : i + 1], (8, 128))

    def panel(p, carry):
        w = [
            [a_ref[8 * t : 8 * t + 8, 128 * h : 128 * h + 128] for h in range(halves)]
            for t in range(tiles)
        ]
        for base in range(0, PB, SB):
            first, last = base // 8, (base + SB) // 8
            cols = [
                {
                    t: jnp.broadcast_to(w[t][0][:, base + j : base + j + 1], (8, 128))
                    for t in range(first, tiles)
                }
                for j in range(SB)
            ]
            inside = (lane8 >= base) & (lane8 < base + SB)
            for t in range(tiles):
                fresh = jnp.where(lane8 == sub8 + 8 * t, 1.0, 0.0) if first <= t < last else 0.0
                w[t][0] = jnp.where(inside, fresh, w[t][0])
            for k in range(SB):
                tk, sk = divmod(base + k, 8)
                r = lax.rsqrt(wide(cols[k][tk], sk))
                m = {t: cols[k][t] * r for t in range(tk, tiles)}
                m[tk] = jnp.where(sub8 > sk, m[tk], 0.0)
                for j in range(k + 1, SB):
                    c = wide(cols[j][tk], sk) * r
                    for t in range(tk, tiles):
                        cols[j][t] = cols[j][t] - m[t] * c
                for h in range(halves):
                    u = wide(w[tk][h], sk) * r
                    for t in range(tk, tiles):
                        w[t][h] = w[t][h] - m[t] * u
                    w[tk][h] = jnp.where(sub8 == sk, u, w[tk][h])
        done = jnp.concatenate([jnp.concatenate(r, axis=1) for r in w], axis=0)
        placed = pltpu.roll(done, p * PB, 1)
        out_ref[pl.ds(pl.multiple_of(p * PB, PB), PB), :] = jnp.where(
            lane < (p + 1) * PB, placed, 0.0
        )
        turned = pltpu.roll(done, n - PB, 1)
        rest = pltpu.roll(jnp.where(lane_rest < PB, 0.0, a_ref[PB:n, :]), n - PB, 1)
        step = lax.dot_general(
            turned, turned, (((0,), (0,)), ((), ())), precision=HI, preferred_element_type=F32
        )
        a_ref[0 : n - PB, :] = rest - step[0 : n - PB]
        return carry

    lax.fori_loop(0, n // PB, panel, 0)


def kernel(
    vals_hbm, slot_hbm, omega_hbm, count_ref,
    basis_ref, proj_ref, core_ref,
    vals_ref, slot_ref, omega_ref,
    part, r1, r2, own, s_all, pick, ready, a_all, meta,
    pair, g_send, g_recv, z_near, z_far, g_all,
    gram, linv, prod, strip, code1, unit1, code2, unit2, w1, c1, w2, c2,
    load_sem, send_sem, r1_sem, r2_sem, s_sem, sib_sem, a_sem, m_sem, pick_sem, ready_sem,
    pair_sem, g_sem, near_sem, far_sem, ag_sem, half_sem, w1_sem, c1_sem, w2_sem, c2_sem,
):
    row, col = lax.axis_index("row"), lax.axis_index("col")
    z, y = row // NY, row % NY
    x, k = col // NK, col % NK
    sib = 1 - k
    q = y * NX + x
    pending = []

    def at(zz, yy, xx, kk):
        return (zz * NY + yy, xx * NK + kk)

    def plane(qq):
        return at(z, qq // NX, qq % NX, k)

    to_sib = at(z, y, x, sib)

    def copy(src, dst, recv_sem, device):
        return pltpu.make_async_remote_copy(
            src_ref=src, dst_ref=dst, send_sem=send_sem, recv_sem=recv_sem,
            device_id=device, device_id_type=MESH,
        )

    def go(c):
        c.start()
        pending.append(c.wait_send)

    barrier = pltpu.get_barrier_semaphore()

    def greet(device):
        pl.semaphore_signal(barrier, inc=1, device_id=device, device_id_type=MESH)

    reach = (6, -6, 5, -5, 4, -4, 3, -3, 2, -2, 1, -1)
    for j in reach:
        greet(at((z + j + NZ) % NZ, y, x, k))
    for j in range(1, NQ):
        greet(plane((q + j) % NQ))
    greet(to_sib)

    pairs = ((slot_hbm, slot_ref), (vals_hbm, vals_ref), (omega_hbm, omega_ref))
    loads = [pltpu.make_async_copy(a, b, load_sem.at[i]) for i, (a, b) in enumerate(pairs)]
    for load in loads:
        load.start()
    for load in loads:
        load.wait()

    col_blocks = omega_ref.shape[0]
    slots = vals_ref.shape[0]
    row_of, live, prods = [], [], []
    for b in range(slots):
        slot = slot_ref[0, b]
        on = count_ref[0, 0] > b
        row_of.append(slot // col_blocks)
        live.append(jnp.where(on, 1.0, 0.0).astype(F32))
        picked = omega_ref[pl.ds(slot % col_blocks, 1)].reshape(BS, RANK)
        prods.append(jnp.dot(vals_ref[b], picked, preferred_element_type=F32))
        a_all[pl.ds(y, 1), b] = (vals_ref[b] * live[b].astype(jnp.bfloat16))[None]
        meta[pl.ds(y, 1), b] = jnp.full(
            (1,) + meta.shape[2:], jnp.where(on, slot % col_blocks, -1), jnp.int32
        )

    def fill(kk):
        for xx in range(NX):
            block = xx * NK + kk
            total = None
            for b in range(slots):
                term = prods[b] * (jnp.where(row_of[b] == block, 1.0, 0.0).astype(F32) * live[b])
                total = term if total is None else total + term
            part[pl.ds(kk, 1), xx] = total[None]

    fill(sib)
    pl.semaphore_wait(barrier, NQ + len(reach))

    def sib_copy(xx):
        return copy(part.at[sib, xx], r1.at[xx], r1_sem.at[xx], to_sib)

    def x_copy(d):
        xx = (x + d) % NX
        return copy(part.at[k, xx], r2.at[d - 1], r2_sem.at[d - 1], at(z, y, xx, k))

    order = (2, 1, 3, 0)
    for d in order:
        go(sib_copy((x + d) % NX))
    fill(k)
    for d in order:
        xx = (x + d) % NX
        sib_copy(xx).wait_recv()
        part[pl.ds(k, 1), pl.ds(xx, 1)] = (
            part[pl.ds(k, 1), pl.ds(xx, 1)] + r1[pl.ds(xx, 1)][None]
        )
        if d:
            go(x_copy(d))

    def a_copies(d):
        to = at(z, (y + d) % NY, x, k)
        return (
            copy(a_all.at[y], a_all.at[y], a_sem.at[d - 1], to),
            copy(meta.at[y], meta.at[y], m_sem.at[d - 1], to),
        )

    for d in (2, 1, 3):
        for c in a_copies(d):
            go(c)
    for d in (1, 3, 2):
        x_copy(d).wait_recv()
    own[...] = (
        part[pl.ds(k, 1), pl.ds(x, 1)].reshape(BS, RANK) + r2[0] + r2[1] + r2[2]
    )

    def gram_half(u, rows):
        n = rows.shape[0]
        pair[u, pl.ds(k, 1), 0:n] = rows[None]
        mine = pair.at[u, k, pl.ds(0, n)]
        swap = copy(mine, mine, pair_sem.at[u], to_sib)
        go(swap)
        copy(mine, pair.at[u, sib, pl.ds(0, n)], pair_sem.at[u], to_sib).wait_recv()
        lanes = pl.ds(pl.multiple_of(k * HALF, HALF), HALF)
        term = None
        for kk in range(NK):
            one = lax.dot_general(
                pair[u, kk, pl.ds(0, n), lanes], pair[u, kk, 0:n], (((0,), (0,)), ((), ())),
                precision=HI, preferred_element_type=F32,
            )
            term = one if term is None else term + one
        g_send[u] = term.reshape(NQ, PIECE, RANK)
        for j in range(1, NQ):
            qq = (q + j) % NQ
            go(copy(g_send.at[u, qq], g_recv.at[u, q], g_sem.at[u], plane(qq)))
        g_recv[u, pl.ds(q, 1)] = g_send[u, pl.ds(q, 1)]

    def arrived(buffer, sem):
        copy(buffer, buffer, sem, to_sib).wait_recv()

    group, member = z // NG, z % NG
    way, reach0 = member // 2 * 2 - 1, 4 - member * (3 - member)

    def reduce_plane(u):
        arrived(g_recv.at[u, pl.ds(0, NQ - 1)], g_sem.at[u])
        total = g_recv[u, 0]
        for i in range(1, NQ):
            total = total + g_recv[u, i]
        z_near[u, pl.ds(member, 1)] = total[None]
        mine = z_near.at[u, member]
        for j in range(1, NG):
            near = group * NG + (member + j) % NG
            go(copy(mine, mine, near_sem.at[u], at(near, y, x, k)))

    def reduce_near(u):
        arrived(z_near.at[u, pl.ds(0, NG - 1)], near_sem.at[u])
        total = z_near[u, 0]
        for i in range(1, NG):
            total = total + z_near[u, i]
        z_far[u, pl.ds(group, 1)] = total[None]
        mine = z_far.at[u, group]
        for j in (2, 1, 0):
            far = (z + way * (reach0 + j) + NZ) % NZ
            go(copy(mine, mine, far_sem.at[u], at(far, y, x, k)))

    def reduce_far(u):
        arrived(z_far.at[u, pl.ds(0, NZ // NG - 1)], far_sem.at[u])
        total = z_far[u, 0]
        for i in range(1, NZ // NG):
            total = total + z_far[u, i]
        g_all[u, pl.ds(k, 1), pl.ds(q, 1)] = total[None, None]
        mine = g_all.at[u, k, q]
        for j in range(1, NQ):
            go(copy(mine, mine, ag_sem.at[u], plane((q + j) % NQ)))

    def gather_plane(u):
        arrived(g_all.at[u, k, pl.ds(0, NQ - 1)], ag_sem.at[u])
        go(copy(g_all.at[u, k], g_all.at[u, k], half_sem.at[u], to_sib))
        copy(g_all.at[u, k], g_all.at[u, sib], half_sem.at[u], to_sib).wait_recv()
        return g_all[u].reshape(RANK, RANK)

    gram_half(0, own[...])

    parts = 2
    depth = BS // parts

    def s_copy(d, i):
        rows = pl.ds(i * depth, depth)
        return copy(
            own.at[rows], s_all.at[k, x, rows], s_sem.at[d - 1, i], at(z, y, (x + d) % NX, k)
        )

    def s_arrival(d, i):
        rows = pl.ds(i * depth, depth)
        return copy(
            own.at[rows], s_all.at[k, (x + NX - d) % NX, rows], s_sem.at[d - 1, i], to_sib
        )

    def pick_copy(d):
        return copy(pick.at[y], pick.at[y], pick_sem.at[d - 1], at(z, (y + d) % NY, x, k))

    def pick_arrival(d):
        yy = (y + NY - d) % NY
        return copy(pick.at[y], pick.at[yy], pick_sem.at[d - 1], at(z, yy, x, k))

    s_all[pl.ds(k, 1), pl.ds(x, 1)] = own[...][None, None]
    reduce_plane(0)
    for d in (2, 1, 3):
        go(s_copy(d, 0))
    reduce_near(0)
    for d in (2, 1, 3):
        go(s_copy(d, 1))
    reduce_far(0)
    for d in (1, 3, 2):
        for i in range(parts):
            s_arrival(d, i).wait_recv()
    go(copy(s_all.at[k], s_all.at[k], sib_sem, to_sib))
    copy(s_all.at[k], s_all.at[sib], sib_sem, to_sib).wait_recv()
    for b in range(slots):
        rows = s_all[pl.ds(row_of[b] % NK, 1), pl.ds(row_of[b] // NK, 1)]
        pick[pl.ds(y, 1), b] = rows.reshape(1, BS, RANK)
    gram[...] = gather_plane(0) * (1.0 / (BS * RB * NY * NZ))

    for d in (1, 3):
        go(pick_copy(d))
    inverse_factor(gram, linv)

    def basis_rows(rows):
        return lax.dot_general(
            rows, linv[...], (((1,), (1,)), ((), ())), precision=HI, preferred_element_type=F32
        ).astype(jnp.bfloat16)

    across = (y + 2) % NY
    for b in range(slots):
        ready[pl.ds(y, 1), b] = basis_rows(pick[pl.ds(y, 1), b].reshape(BS, RANK))[None]
    go(copy(ready.at[y], ready.at[y], ready_sem, at(z, across, x, k)))
    basis_ref[...] = basis_rows(own[...])

    def products(yy, formed):
        for b in range(slots):
            if formed:
                rows = ready[pl.ds(yy, 1), b].reshape(BS, RANK)
            else:
                rows = basis_rows(pick[pl.ds(yy, 1), b].reshape(BS, RANK))
            block = a_all[pl.ds(yy, 1), b].reshape(BS, BS)
            prod[pl.ds(yy, 1), b] = lax.dot_general(
                block, rows, (((0,), (0,)), ((), ())), preferred_element_type=F32
            )[None]

    products(y, True)
    for d in (1, 3, 2):
        yy = (y + NY - d) % NY
        to = at(z, yy, x, k)
        copy(a_all.at[y], a_all.at[yy], a_sem.at[d - 1], to).wait_recv()
        copy(meta.at[y], meta.at[yy], m_sem.at[d - 1], to).wait_recv()
        if d == 2:
            copy(ready.at[y], ready.at[yy], ready_sem, to).wait_recv()
        else:
            pick_arrival(d).wait_recv()
        products(yy, d == 2)

    tile = 16
    per_strip = STRIP // tile

    def coded(v):
        top = jnp.maximum(jnp.max(jnp.abs(v), axis=0, keepdims=True), 1e-33)
        return jnp.round(v * (STEPS / top)).astype(jnp.int32).astype(jnp.int16), top * (1.0 / STEPS)

    def value(steps, unit):
        return steps.astype(jnp.int32).astype(F32) * unit

    def place(zz, carry):
        totals = []
        for t in range(per_strip):
            g = zz * (NY * per_strip) + y * per_strip + t
            block, rows = g // (BS // tile), pl.multiple_of(g % (BS // tile) * tile, tile)
            total = jnp.zeros((tile, RANK), F32)
            for yy in range(NY):
                for b in range(slots):
                    here = jnp.concatenate([meta[yy, b] == block] * (RANK // 128), axis=1)
                    total = total + jnp.where(here, prod[yy, b, pl.ds(rows, tile), :], 0.0)
            totals.append(total)
        total = jnp.concatenate(totals, axis=0)
        strip[pl.ds(zz, 1)] = total[None]
        steps, unit = coded(total)
        code1[pl.ds(zz, 1)] = steps[None]
        unit1[pl.ds(zz, 1), :] = unit
        return carry

    lax.fori_loop(0, NZ, place, 0)

    sign = 1 - 2 * k
    near = (1, -1, 2)

    def w1_copy(i, e):
        mid = (z + sign * near[i] + NZ) % NZ
        dest = (mid + FAR[e] + NZ) % NZ
        return copy(code1.at[dest], w1.at[e, i], w1_sem.at[e, i], at(mid, y, x, k))

    def c1_copy(i):
        return copy(unit1, c1.at[i], c1_sem.at[i], at((z + sign * near[i] + NZ) % NZ, y, x, k))

    def w2_copies(e):
        to = at((z + FAR[e] + NZ) % NZ, y, x, k)
        return (
            copy(code2.at[e], w2.at[e], w2_sem.at[e], to),
            copy(unit2.at[e], c2.at[e], c2_sem.at[e], to),
        )

    for i in (2, 0, 1):
        go(c1_copy(i))
    for e in range(4):
        for i in (2, 0, 1):
            go(w1_copy(i, e))
    for i in range(3):
        c1_copy(i).wait_recv()
    for e in range(4):
        for i in range(3):
            w1_copy(i, e).wait_recv()
        dest = (z + FAR[e] + NZ) % NZ
        total = strip[pl.ds(dest, 1)].reshape(STRIP, RANK)
        for i in range(3):
            total = total + value(w1[e, i], c1[i, pl.ds(dest, 1), :])
        code2[e], unit2[e] = coded(total)
        for c in w2_copies(e):
            go(c)
    proj = jnp.zeros((STRIP, RANK), F32)
    for e in range(4):
        for c in w2_copies(e):
            c.wait_recv()
        proj = proj + value(w2[e], c2[e])
    proj = proj * (1.0 / 256.0)
    proj_ref[0] = proj

    gram_half(1, proj)
    reduce_plane(1)
    reduce_near(1)
    reduce_far(1)
    core_ref[...] = gather_plane(1) / float(col_blocks * BS * NX * NK)

    for wait in pending:
        wait()


def body(block_vals, block_slot, block_count, omega):
    slots = block_vals.shape[0]
    vmem = pl.BlockSpec(memory_space=pltpu.VMEM)
    hbm = pl.BlockSpec(memory_space=pltpu.HBM)
    dma = pltpu.SemaphoreType.DMA
    blocks = lambda *lead: pltpu.VMEM((*lead, BS, RANK), F32)
    inputs = [
        pltpu.with_memory_space_constraint(a, pltpu.HBM)
        for a in (block_vals, block_slot.T, omega.reshape(-1, BS, RANK))
    ]
    basis, projected, core = pl.pallas_call(
        kernel,
        out_shape=(
            pltpu.VMEM((BS, RANK), jnp.bfloat16),
            pltpu.VMEM((1, STRIP, RANK), F32),
            pltpu.VMEM((RANK, RANK), F32),
        ),
        in_specs=[hbm] * 3 + [pl.BlockSpec(memory_space=pltpu.SMEM)],
        out_specs=(vmem, vmem, vmem),
        scratch_shapes=[
            pltpu.VMEM(block_vals.shape, block_vals.dtype),
            pltpu.SMEM(block_slot.shape[::-1], jnp.int32),
            pltpu.VMEM((omega.shape[0] // BS, BS, RANK), omega.dtype),
            blocks(NK, NX),
            blocks(NX),
            blocks(NX - 1),
            blocks(),
            blocks(NK, NX),
            blocks(NY, slots),
            pltpu.VMEM((NY, slots, BS, RANK), jnp.bfloat16),
            pltpu.VMEM((NY, slots, BS, BS), jnp.bfloat16),
            pltpu.VMEM((NY, slots, 16, 128), jnp.int32),
            blocks(2, NK),
            pltpu.VMEM((2, NQ, PIECE, RANK), F32),
            pltpu.VMEM((2, NQ, PIECE, RANK), F32),
            pltpu.VMEM((2, NG, PIECE, RANK), F32),
            pltpu.VMEM((2, NZ // NG, PIECE, RANK), F32),
            pltpu.VMEM((2, NK, NQ, PIECE, RANK), F32),
            pltpu.VMEM((RANK, RANK), F32),
            pltpu.VMEM((RANK, RANK), F32),
            blocks(NY, slots),
            pltpu.VMEM((NZ, STRIP, RANK), F32),
            pltpu.VMEM((NZ, STRIP, RANK), jnp.int16),
            pltpu.VMEM((NZ, RANK), F32),
            pltpu.VMEM((4, STRIP, RANK), jnp.int16),
            pltpu.VMEM((4, 1, RANK), F32),
            pltpu.VMEM((4, 3, STRIP, RANK), jnp.int16),
            pltpu.VMEM((3, NZ, RANK), F32),
            pltpu.VMEM((4, STRIP, RANK), jnp.int16),
            pltpu.VMEM((4, 1, RANK), F32),
            dma((3,)), dma,
            dma((NX,)), dma((NX - 1,)), dma((NX - 1, 2)), dma, dma((NY - 1,)), dma((NY - 1,)), dma((NY - 1,)), dma,
            dma((2,)), dma((2,)), dma((2,)), dma((2,)), dma((2,)), dma((2,)), dma((4, 3)), dma((3,)), dma((4,)), dma((4,)),
        ],
        compiler_params=pltpu.CompilerParams(
            collective_id=0, has_side_effects=True, vmem_limit_bytes=60 * 2**20
        ),
        name="range_basis",
    )(*inputs, block_count)
    return basis, projected, core


def solution(mesh):
    placed = (P("row", "col", None), P("row", "col"), P("row", "col"), P("col", None))
    return jax.shard_map(
        body,
        mesh=mesh,
        in_specs=placed,
        out_specs=(P(("row", "col"), None), P("col", "row", None), P()),
        check_vma=False,
    )
```

```python
import functools

import jax
import jax.numpy as jnp
from jax import lax
from jax.experimental import pallas as pl
from jax.experimental.pallas import tpu as pltpu
from jax.sharding import PartitionSpec as P

MESH = pl.DeviceIdType.MESH
HI = lax.Precision.HIGHEST
F32 = jnp.float32

RB = 8
BS = 128
RANK = 256
NY, NZ, NX, NK = 4, 16, 4, 2
NQ = NY * NX
HALF = RANK // NK
PIECE = HALF // NQ
STRIP = 48
PB, SB = 64, 16
NG = 4
STEPS = 32767.0
FAR = (6, -6, 2, -2)


def inverse_factor(a_ref, out_ref):
    n = a_ref.shape[0]
    lane = lax.broadcasted_iota(jnp.int32, (PB, n), 1)
    lane8 = lax.broadcasted_iota(jnp.int32, (8, 128), 1)
    sub8 = lax.broadcasted_iota(jnp.int32, (8, 128), 0)
    lane_rest = lax.broadcasted_iota(jnp.int32, (n - PB, n), 1)
    tiles, halves = PB // 8, n // 128

    def wide(v, i):
        return jnp.broadcast_to(v[i : i + 1], (8, 128))

    def panel(p, carry):
        w = [
            [a_ref[8 * t : 8 * t + 8, 128 * h : 128 * h + 128] for h in range(halves)]
            for t in range(tiles)
        ]
        for base in range(0, PB, SB):
            first, last = base // 8, (base + SB) // 8
            cols = [
                {
                    t: jnp.broadcast_to(w[t][0][:, base + j : base + j + 1], (8, 128))
                    for t in range(first, tiles)
                }
                for j in range(SB)
            ]
            inside = (lane8 >= base) & (lane8 < base + SB)
            for t in range(tiles):
                fresh = jnp.where(lane8 == sub8 + 8 * t, 1.0, 0.0) if first <= t < last else 0.0
                w[t][0] = jnp.where(inside, fresh, w[t][0])
            for k in range(SB):
                tk, sk = divmod(base + k, 8)
                r = lax.rsqrt(wide(cols[k][tk], sk))
                m = {t: cols[k][t] * r for t in range(tk, tiles)}
                m[tk] = jnp.where(sub8 > sk, m[tk], 0.0)
                for j in range(k + 1, SB):
                    c = wide(cols[j][tk], sk) * r
                    for t in range(tk, tiles):
                        cols[j][t] = cols[j][t] - m[t] * c
                for h in range(halves):
                    u = wide(w[tk][h], sk) * r
                    for t in range(tk, tiles):
                        w[t][h] = w[t][h] - m[t] * u
                    w[tk][h] = jnp.where(sub8 == sk, u, w[tk][h])
        done = jnp.concatenate([jnp.concatenate(r, axis=1) for r in w], axis=0)
        placed = pltpu.roll(done, p * PB, 1)
        out_ref[pl.ds(pl.multiple_of(p * PB, PB), PB), :] = jnp.where(
            lane < (p + 1) * PB, placed, 0.0
        )

        @pl.when(p < n // PB - 1)
        def _():
            turned = pltpu.roll(done, n - PB, 1)
            rest = pltpu.roll(jnp.where(lane_rest < PB, 0.0, a_ref[PB:n, :]), n - PB, 1)
            step = lax.dot_general(
                turned, turned, (((0,), (0,)), ((), ())), precision=HI, preferred_element_type=F32
            )
            a_ref[0 : n - PB, :] = rest - step[0 : n - PB]

        return carry

    lax.fori_loop(0, n // PB, panel, 0)


def kernel(
    vals_hbm, slot_hbm, omega_hbm, count_ref,
    basis_ref, proj_ref, core_ref,
    vals_ref, slot_ref, omega_ref,
    part, r1, relay, r2, own, s_all, pick, ready, a_all, meta,
    pair0, pair1, g_send, g_recv, z_near, z_far, g_all,
    gram, linv, prod, strip, code1, unit1, code2, unit2, w1, c1, w2, c2,
    beyond_sem, load_sem, send_sem, r1_sem, relay_sem, r2_sem, s_sem, sib_sem, a_sem, m_sem, pick_sem, ready_sem,
    pair_sem, g_sem, near_sem, far_sem, ag_sem, half_sem, w1_sem, c1_sem, w2_sem, c2_sem,
):
    row, col = lax.axis_index("row"), lax.axis_index("col")
    z, y = lax.div(row, NY), lax.rem(row, NY)
    x, k = lax.div(col, NK), lax.rem(col, NK)
    sib = 1 - k
    q = y * NX + x
    pending = []
    pairs = (pair0, pair1)

    def around(i, n):
        return lax.rem(i + n, n)

    def at(zz, yy, xx, kk):
        return (zz * NY + yy, xx * NK + kk)

    def plane(qq):
        return at(z, lax.div(qq, NX), lax.rem(qq, NX), k)

    to_sib = at(z, y, x, sib)

    def copy(src, dst, recv_sem, device):
        return pltpu.make_async_remote_copy(
            src_ref=src, dst_ref=dst, send_sem=send_sem, recv_sem=recv_sem,
            device_id=device, device_id_type=MESH,
        )

    def go(c):
        c.start()
        pending.append(c.wait_send)

    def flush():
        while pending:
            pending.pop(0)()

    moves = ((slot_hbm, slot_ref), (vals_hbm, vals_ref), (omega_hbm, omega_ref))
    loads = [pltpu.make_async_copy(a, b, load_sem.at[i]) for i, (a, b) in enumerate(moves)]
    for load in loads:
        load.start()

    barrier = pltpu.get_barrier_semaphore()

    def greet(device):
        pl.semaphore_signal(barrier, inc=1, device_id=device, device_id_type=MESH)

    reach = (3, -3, 2, -2, 1, -1)
    for j in reach:
        greet(at(around(z + j, NZ), y, x, k))
    for j in range(1, NQ):
        greet(plane(around(q + j, NQ)))
    greet(to_sib)

    for load in loads:
        load.wait()

    col_blocks = omega_ref.shape[0]
    slots = vals_ref.shape[0]
    row_of, live, prods = [], [], []
    for b in range(slots):
        slot = slot_ref[0, b]
        on = count_ref[0, 0] > b
        row_of.append(lax.div(slot, col_blocks))
        live.append(jnp.where(on, 1.0, 0.0).astype(F32))
        picked = omega_ref[pl.ds(lax.rem(slot, col_blocks), 1)].reshape(BS, RANK)
        prods.append(jnp.dot(vals_ref[b], picked, preferred_element_type=F32))
        a_all[pl.ds(y, 1), b] = (vals_ref[b] * live[b].astype(jnp.bfloat16))[None]
        meta[pl.ds(y, 1), b] = jnp.full(
            (1,) + meta.shape[2:], jnp.where(on, lax.rem(slot, col_blocks), -1), jnp.int32
        )

    def fill(kk):
        for xx in range(NX):
            block = xx * NK + kk
            total = None
            for b in range(slots):
                term = prods[b] * (jnp.where(row_of[b] == block, 1.0, 0.0).astype(F32) * live[b])
                total = term if total is None else total + term
            part[pl.ds(kk, 1), xx] = total[None]

    fill(sib)
    pl.semaphore_wait(barrier, NQ + len(reach))
    for j in (3, -3):
        to = at(around(z + j, NZ), y, x, k)
        pl.semaphore_signal(beyond_sem, inc=1, device_id=to, device_id_type=MESH)

    def sib_copy(xx):
        return copy(part.at[sib, xx], r1.at[xx], r1_sem.at[xx], to_sib)

    half = BS // 2
    sides = (1, -1)

    def rows_of(i):
        return pl.ds(i * half, half)

    def relay_copy(i):
        src = part.at[k, around(x + 2, NX), rows_of(i)]
        return copy(src, relay.at[i], relay_sem.at[i], at(z, y, around(x + sides[i], NX), k))

    def x_copy(i, r):
        xx = around(x + sides[i], NX)
        src = part.at[k, xx, rows_of(r)]
        return copy(src, r2.at[i, rows_of(r)], r2_sem.at[i, r], at(z, y, xx, k))

    def a_copies(d):
        to = at(z, around(y + d, NY), x, k)
        return (
            copy(a_all.at[y], a_all.at[y], a_sem.at[d - 1], to),
            copy(meta.at[y], meta.at[y], m_sem.at[d - 1], to),
        )

    def join(d):
        xx = around(x + d, NX)
        sib_copy(xx).wait_recv()
        part[pl.ds(k, 1), pl.ds(xx, 1)] = (
            part[pl.ds(k, 1), pl.ds(xx, 1)] + r1[pl.ds(xx, 1)][None]
        )

    for d in (2, 1, 3, 0):
        go(sib_copy(around(x + d, NX)))
    fill(k)
    join(2)
    for i in range(2):
        go(relay_copy(i))
    for i in range(2):
        join(sides[i])
        go(x_copy(i, 1 - i))
    join(0)
    for d in (2, 1, 3):
        for c in a_copies(d):
            go(c)
    for i in range(2):
        relay_copy(i).wait_recv()
        at_rows = (pl.ds(k, 1), pl.ds(around(x + sides[i], NX), 1), rows_of(i))
        part[at_rows] = part[at_rows] + relay[i][None, None]
        go(x_copy(i, i))
    for i in range(2):
        for r in range(2):
            x_copy(i, r).wait_recv()
    own[...] = part[pl.ds(k, 1), pl.ds(x, 1)].reshape(BS, RANK) + r2[0] + r2[1]

    def gram_half(u, rows):
        pair = pairs[u]
        pair[pl.ds(k, 1)] = rows[None]
        go(copy(pair.at[k], pair.at[k], pair_sem.at[u], to_sib))
        copy(pair.at[k], pair.at[sib], pair_sem.at[u], to_sib).wait_recv()
        n = NK * rows.shape[0]
        lanes = pl.ds(pl.multiple_of(k * HALF, HALF), HALF)
        term = lax.dot_general(
            pair[:, :, lanes].reshape(n, HALF), pair[...].reshape(n, RANK), (((0,), (0,)), ((), ())),
            precision=HI, preferred_element_type=F32,
        )
        g_send[u] = term.reshape(NQ, PIECE, RANK)
        for j in range(1, NQ):
            qq = around(q + j, NQ)
            go(copy(g_send.at[u, qq], g_recv.at[u, q], g_sem.at[u], plane(qq)))
        g_recv[u, pl.ds(q, 1)] = g_send[u, pl.ds(q, 1)]

    def arrived(buffer, sem):
        copy(buffer, buffer, sem, to_sib).wait_recv()

    group, member = lax.div(z, NG), lax.rem(z, NG)
    way, reach0 = lax.div(member, 2) * 2 - 1, 4 - member * (3 - member)

    def reduce_plane(u):
        arrived(g_recv.at[u, pl.ds(0, NQ - 1)], g_sem.at[u])
        total = g_recv[u, 0]
        for i in range(1, NQ):
            total = total + g_recv[u, i]
        z_near[u, pl.ds(member, 1)] = total[None]
        mine = z_near.at[u, member]
        for j in range(1, NG):
            near = group * NG + around(member + j, NG)
            go(copy(mine, mine, near_sem.at[u], at(near, y, x, k)))

    def reduce_near(u):
        arrived(z_near.at[u, pl.ds(0, NG - 1)], near_sem.at[u])
        total = z_near[u, 0]
        for i in range(1, NG):
            total = total + z_near[u, i]
        z_far[u, pl.ds(group, 1)] = total[None]
        mine = z_far.at[u, group]
        if u == 0:
            pl.semaphore_wait(beyond_sem, 2)
        for j in (2, 1, 0):
            far = around(z + way * (reach0 + j), NZ)
            go(copy(mine, mine, far_sem.at[u], at(far, y, x, k)))

    def reduce_far(u):
        arrived(z_far.at[u, pl.ds(0, NZ // NG - 1)], far_sem.at[u])
        total = z_far[u, 0]
        for i in range(1, NZ // NG):
            total = total + z_far[u, i]
        g_all[u, pl.ds(k, 1), pl.ds(q, 1)] = total[None, None]
        mine = g_all.at[u, k, q]
        for j in range(1, NQ):
            go(copy(mine, mine, ag_sem.at[u], plane(around(q + j, NQ))))

    def gather_plane(u):
        flush()
        arrived(g_all.at[u, k, pl.ds(0, NQ - 1)], ag_sem.at[u])
        go(copy(g_all.at[u, k], g_all.at[u, k], half_sem.at[u], to_sib))
        copy(g_all.at[u, k], g_all.at[u, sib], half_sem.at[u], to_sib).wait_recv()
        return g_all[u].reshape(RANK, RANK)

    gram_half(0, own[...])

    parts = 2
    depth = BS // parts

    def s_copy(d, i):
        rows = pl.ds(i * depth, depth)
        return copy(
            own.at[rows], s_all.at[k, x, rows], s_sem.at[d - 1, i], at(z, y, around(x + d, NX), k)
        )

    def s_arrival(d, i):
        rows = pl.ds(i * depth, depth)
        return copy(
            own.at[rows], s_all.at[k, around(x - d, NX), rows], s_sem.at[d - 1, i], to_sib
        )

    early = slots // 2

    def pick_copy(d):
        mine = pick.at[y, pl.ds(0, early)] if d == 2 else pick.at[y]
        return copy(mine, mine, pick_sem.at[d - 1], at(z, around(y + d, NY), x, k))

    def pick_arrival(d):
        yy = around(y - d, NY)
        here = pick.at[yy, pl.ds(0, early)] if d == 2 else pick.at[yy]
        return copy(here, here, pick_sem.at[d - 1], at(z, yy, x, k))

    s_all[pl.ds(k, 1), pl.ds(x, 1)] = own[...][None, None]
    reduce_plane(0)
    for d in (2, 1, 3):
        go(s_copy(d, 0))
    reduce_near(0)
    for d in (2, 1, 3):
        go(s_copy(d, 1))
    reduce_far(0)
    for d in (1, 3, 2):
        for i in range(parts):
            s_arrival(d, i).wait_recv()
    go(copy(s_all.at[k], s_all.at[k], sib_sem, to_sib))
    copy(s_all.at[k], s_all.at[sib], sib_sem, to_sib).wait_recv()
    for b in range(slots):
        rows = s_all[pl.ds(lax.rem(row_of[b], NK), 1), pl.ds(lax.div(row_of[b], NK), 1)]
        pick[pl.ds(y, 1), b] = rows.reshape(1, BS, RANK)
    gram[...] = gather_plane(0) * (1.0 / (BS * RB * NY * NZ))

    for d in (1, 3, 2):
        go(pick_copy(d))
    inverse_factor(gram, linv)

    def basis_rows(rows):
        return lax.dot_general(
            rows, linv[...], (((1,), (1,)), ((), ())), precision=HI, preferred_element_type=F32
        ).astype(jnp.bfloat16)

    def form(yy, lo, hi):
        def one(b, carry):
            rows = basis_rows(pick[pl.ds(yy, 1), pl.ds(b, 1)].reshape(BS, RANK))
            ready[pl.ds(yy, 1), pl.ds(b, 1)] = rows[None, None]
            return carry

        lax.fori_loop(lo, hi, one, 0)

    def products(yy):
        def one(b, carry):
            prod[pl.ds(yy, 1), pl.ds(b, 1)] = lax.dot_general(
                a_all[pl.ds(yy, 1), pl.ds(b, 1)].reshape(BS, BS),
                ready[pl.ds(yy, 1), pl.ds(b, 1)].reshape(BS, RANK),
                (((0,), (0,)), ((), ())), preferred_element_type=F32,
            )[None, None]
            return carry

        lax.fori_loop(0, slots, one, 0)

    def ready_copy(yy):
        late = pl.ds(early, slots - early)
        to = at(z, around(y + 2, NY), x, k)
        return copy(ready.at[yy, late], ready.at[yy, late], ready_sem, to)

    def each(i, carry):
        d = jnp.where(i == 3, 2, jnp.where(i == 2, 3, i))
        yy = around(y - d, NY)

        @pl.when(i > 0)
        def _():
            to = at(z, yy, x, k)
            copy(a_all.at[y], a_all.at[yy], a_sem.at[d - 1], to).wait_recv()
            copy(meta.at[y], meta.at[yy], m_sem.at[d - 1], to).wait_recv()

        @pl.when((i == 1) | (i == 2))
        def _():
            copy(pick.at[y], pick.at[yy], pick_sem.at[d - 1], to_sib).wait_recv()

        @pl.when(i == 3)
        def _():
            pick_arrival(2).wait_recv()

        @pl.when(i < 3)
        def _():
            form(yy, early, slots)

        @pl.when(i == 0)
        def _():
            ready_copy(y).start()

        form(yy, 0, early)

        @pl.when(i == 0)
        def _():
            basis_ref[...] = basis_rows(own[...])

        @pl.when(i == 3)
        def _():
            ready_copy(yy).wait_recv()

        products(yy)
        return carry

    lax.fori_loop(0, NY, each, 0)
    pending.append(ready_copy(y).wait_send)

    tile = 16
    per_strip = STRIP // tile

    def coded(v):
        top = jnp.maximum(jnp.max(jnp.abs(v), axis=0, keepdims=True), 1e-33)
        return jnp.round(v * (STEPS / top)).astype(jnp.int32).astype(jnp.int16), top * (1.0 / STEPS)

    def value(steps, unit):
        return steps.astype(jnp.int32).astype(F32) * unit

    def place(zz, carry):
        totals = []
        for t in range(per_strip):
            g = zz * (NY * per_strip) + y * per_strip + t
            block = lax.div(g, BS // tile)
            rows = pl.multiple_of(lax.rem(g, BS // tile) * tile, tile)
            total = jnp.zeros((tile, RANK), F32)
            for yy in range(NY):
                for b in range(slots):
                    here = jnp.concatenate([meta[yy, b] == block] * (RANK // 128), axis=1)
                    total = total + jnp.where(here, prod[yy, b, pl.ds(rows, tile), :], 0.0)
            totals.append(total)
        total = jnp.concatenate(totals, axis=0)
        strip[pl.ds(zz, 1)] = total[None]
        steps, unit = coded(total)
        code1[pl.ds(zz, 1)] = steps[None]
        unit1[pl.ds(zz, 1), :] = unit
        return carry

    lax.fori_loop(0, NZ, place, 0)

    sign = 1 - 2 * k
    near = (1, -1, 2)

    def w1_copy(i, e):
        mid = around(z + sign * near[i], NZ)
        dest = around(mid + FAR[e], NZ)
        return copy(code1.at[dest], w1.at[e, i], w1_sem.at[e, i], at(mid, y, x, k))

    def c1_copy(i):
        return copy(unit1, c1.at[i], c1_sem.at[i], at(around(z + sign * near[i], NZ), y, x, k))

    def w2_copies(e):
        to = at(around(z + FAR[e], NZ), y, x, k)
        return (
            copy(code2.at[e], w2.at[e], w2_sem.at[e], to),
            copy(unit2.at[e], c2.at[e], c2_sem.at[e], to),
        )

    for i in (2, 0, 1):
        go(c1_copy(i))
    for e in range(4):
        for i in (2, 0, 1):
            go(w1_copy(i, e))
    for i in range(3):
        c1_copy(i).wait_recv()
    for e in range(4):
        for i in range(3):
            w1_copy(i, e).wait_recv()
        dest = around(z + FAR[e], NZ)
        total = strip[pl.ds(dest, 1)].reshape(STRIP, RANK)
        for i in range(3):
            total = total + value(w1[e, i], c1[i, pl.ds(dest, 1), :])
        code2[e], unit2[e] = coded(total)
        for c in w2_copies(e):
            go(c)
    proj = jnp.zeros((STRIP, RANK), F32)
    for e in range(4):
        for c in w2_copies(e):
            c.wait_recv()
        proj = proj + value(w2[e], c2[e])
    proj = proj * (1.0 / 256.0)
    proj_ref[0] = proj

    gram_half(1, proj)
    reduce_plane(1)
    reduce_near(1)
    reduce_far(1)
    core_ref[...] = gather_plane(1) / float(col_blocks * BS * NX * NK)

    flush()


def body(block_vals, block_slot, block_count, omega):
    slots = block_vals.shape[0]
    vmem = pl.BlockSpec(memory_space=pltpu.VMEM)
    hbm = pl.BlockSpec(memory_space=pltpu.HBM)
    dma = pltpu.SemaphoreType.DMA
    blocks = lambda *lead: pltpu.VMEM((*lead, BS, RANK), F32)
    inputs = [
        pltpu.with_memory_space_constraint(a, pltpu.HBM)
        for a in (block_vals, block_slot.T, omega.reshape(-1, BS, RANK))
    ]
    basis, projected, core = pl.pallas_call(
        kernel,
        out_shape=(
            pltpu.VMEM((BS, RANK), jnp.bfloat16),
            pltpu.VMEM((1, STRIP, RANK), F32),
            pltpu.VMEM((RANK, RANK), F32),
        ),
        in_specs=[hbm] * 3 + [pl.BlockSpec(memory_space=pltpu.SMEM)],
        out_specs=(vmem, vmem, vmem),
        scratch_shapes=[
            pltpu.VMEM(block_vals.shape, block_vals.dtype),
            pltpu.SMEM(block_slot.shape[::-1], jnp.int32),
            pltpu.VMEM((omega.shape[0] // BS, BS, RANK), omega.dtype),
            blocks(NK, NX),
            blocks(NX),
            pltpu.VMEM((2, BS // 2, RANK), F32),
            blocks(2),
            blocks(),
            blocks(NK, NX),
            blocks(NY, slots),
            pltpu.VMEM((NY, slots, BS, RANK), jnp.bfloat16),
            pltpu.VMEM((NY, slots, BS, BS), jnp.bfloat16),
            pltpu.VMEM((NY, slots, 16, 128), jnp.int32),
            blocks(NK),
            pltpu.VMEM((NK, STRIP, RANK), F32),
            pltpu.VMEM((2, NQ, PIECE, RANK), F32),
            pltpu.VMEM((2, NQ, PIECE, RANK), F32),
            pltpu.VMEM((2, NG, PIECE, RANK), F32),
            pltpu.VMEM((2, NZ // NG, PIECE, RANK), F32),
            pltpu.VMEM((2, NK, NQ, PIECE, RANK), F32),
            pltpu.VMEM((RANK, RANK), F32),
            pltpu.VMEM((RANK, RANK), F32),
            blocks(NY, slots),
            pltpu.VMEM((NZ, STRIP, RANK), F32),
            pltpu.VMEM((NZ, STRIP, RANK), jnp.int16),
            pltpu.VMEM((NZ, RANK), F32),
            pltpu.VMEM((4, STRIP, RANK), jnp.int16),
            pltpu.VMEM((4, 1, RANK), F32),
            pltpu.VMEM((4, 3, STRIP, RANK), jnp.int16),
            pltpu.VMEM((3, NZ, RANK), F32),
            pltpu.VMEM((4, STRIP, RANK), jnp.int16),
            pltpu.VMEM((4, 1, RANK), F32),
            pltpu.SemaphoreType.REGULAR,
            dma((3,)), dma,
            dma((NX,)), dma((2,)), dma((2, 2)), dma((NX - 1, 2)), dma, dma((NY - 1,)), dma((NY - 1,)), dma((NY - 1,)), dma,
            dma((2,)), dma((2,)), dma((2,)), dma((2,)), dma((2,)), dma((2,)), dma((4, 3)), dma((3,)), dma((4,)), dma((4,)),
        ],
        compiler_params=pltpu.CompilerParams(
            collective_id=0, has_side_effects=True, vmem_limit_bytes=60 * 2**20
        ),
        name="range_basis",
    )(*inputs, block_count)
    return basis, projected, core


def solution(mesh):
    placed = (P("row", "col", None), P("row", "col"), P("row", "col"), P("col", None))
    return jax.shard_map(
        body,
        mesh=mesh,
        in_specs=placed,
        out_specs=(P(("row", "col"), None), P("col", "row", None), P()),
        check_vma=False,
    )
```

```python
import functools

import jax
import jax.numpy as jnp
from jax import lax
from jax.experimental import pallas as pl
from jax.experimental.pallas import tpu as pltpu
from jax.sharding import PartitionSpec as P

MESH = pl.DeviceIdType.MESH
HI = lax.Precision.HIGHEST
F32 = jnp.float32

RB = 8
BS = 128
RANK = 256
NY, NZ, NX, NK = 4, 16, 4, 2
NQ = NY * NX
HALF = RANK // NK
PIECE = HALF // NQ
STRIP = 48
PB, SB = 64, 16
NG = 4
STEPS = 32767.0
FAR = (6, -6, 2, -2)


def inverse_factor(a_ref, out_ref):
    n = a_ref.shape[0]
    lane = lax.broadcasted_iota(jnp.int32, (PB, n), 1)
    lane8 = lax.broadcasted_iota(jnp.int32, (8, 128), 1)
    sub8 = lax.broadcasted_iota(jnp.int32, (8, 128), 0)
    lane_rest = lax.broadcasted_iota(jnp.int32, (n - PB, n), 1)
    tiles, halves = PB // 8, n // 128

    def wide(v, i):
        return jnp.broadcast_to(v[i : i + 1], (8, 128))

    def panel(p, carry):
        w = [
            [a_ref[8 * t : 8 * t + 8, 128 * h : 128 * h + 128] for h in range(halves)]
            for t in range(tiles)
        ]
        for base in range(0, PB, SB):
            first, last = base // 8, (base + SB) // 8
            cols = [
                {
                    t: jnp.broadcast_to(w[t][0][:, base + j : base + j + 1], (8, 128))
                    for t in range(first, tiles)
                }
                for j in range(SB)
            ]
            inside = (lane8 >= base) & (lane8 < base + SB)
            for t in range(tiles):
                fresh = jnp.where(lane8 == sub8 + 8 * t, 1.0, 0.0) if first <= t < last else 0.0
                w[t][0] = jnp.where(inside, fresh, w[t][0])
            for k in range(SB):
                tk, sk = divmod(base + k, 8)
                r = lax.rsqrt(wide(cols[k][tk], sk))
                m = {t: cols[k][t] * r for t in range(tk, tiles)}
                m[tk] = jnp.where(sub8 > sk, m[tk], 0.0)
                for j in range(k + 1, SB):
                    c = wide(cols[j][tk], sk) * r
                    for t in range(tk, tiles):
                        cols[j][t] = cols[j][t] - m[t] * c
                for h in range(halves):
                    u = wide(w[tk][h], sk) * r
                    for t in range(tk, tiles):
                        w[t][h] = w[t][h] - m[t] * u
                    w[tk][h] = jnp.where(sub8 == sk, u, w[tk][h])
        done = jnp.concatenate([jnp.concatenate(r, axis=1) for r in w], axis=0)
        placed = pltpu.roll(done, p * PB, 1)
        out_ref[pl.ds(pl.multiple_of(p * PB, PB), PB), :] = jnp.where(
            lane < (p + 1) * PB, placed, 0.0
        )

        @pl.when(p < n // PB - 1)
        def _():
            turned = pltpu.roll(done, n - PB, 1)
            rest = pltpu.roll(jnp.where(lane_rest < PB, 0.0, a_ref[PB:n, :]), n - PB, 1)
            step = lax.dot_general(
                turned, turned, (((0,), (0,)), ((), ())), precision=HI, preferred_element_type=F32
            )
            a_ref[0 : n - PB, :] = rest - step[0 : n - PB]

        return carry

    lax.fori_loop(0, n // PB, panel, 0)


def kernel(
    vals_hbm, slot_hbm, omega_hbm, count_ref,
    basis_ref, proj_ref, core_ref,
    vals_ref, slot_ref, omega_ref,
    part, r1, relay, r2, own, s_all, pick, ready, a_all, meta,
    pair0, pair1, g_send, g_recv, z_near, z_far, g_all,
    gram, linv, factor, prod, strip, code1, unit1, code2, unit2, w1, c1, w2, c2,
    beyond_sem, load_sem, send_sem, r1_sem, relay_sem, r2_sem, s_sem, sib_sem, a_sem, m_sem, pick_sem, ready_sem,
    pair_sem, g_sem, near_sem, far_sem, ag_sem, half_sem, w1_sem, c1_sem, w2_sem, c2_sem,
):
    row, col = lax.axis_index("row"), lax.axis_index("col")
    z, y = lax.div(row, NY), lax.rem(row, NY)
    x, k = lax.div(col, NK), lax.rem(col, NK)
    sib = 1 - k
    q = y * NX + x
    pending = []
    pairs = (pair0, pair1)

    def around(i, n):
        return lax.rem(i + n, n)

    def at(zz, yy, xx, kk):
        return (zz * NY + yy, xx * NK + kk)

    def plane(qq):
        return at(z, lax.div(qq, NX), lax.rem(qq, NX), k)

    to_sib = at(z, y, x, sib)

    def copy(src, dst, recv_sem, device):
        return pltpu.make_async_remote_copy(
            src_ref=src, dst_ref=dst, send_sem=send_sem, recv_sem=recv_sem,
            device_id=device, device_id_type=MESH,
        )

    def go(c):
        c.start()
        pending.append(c.wait_send)

    def flush():
        while pending:
            pending.pop(0)()

    moves = ((slot_hbm, slot_ref), (vals_hbm, vals_ref), (omega_hbm, omega_ref))
    loads = [pltpu.make_async_copy(a, b, load_sem.at[i]) for i, (a, b) in enumerate(moves)]
    for load in loads:
        load.start()

    barrier = pltpu.get_barrier_semaphore()

    def greet(device):
        pl.semaphore_signal(barrier, inc=1, device_id=device, device_id_type=MESH)

    reach = (3, -3, 2, -2, 1, -1)
    for j in reach:
        greet(at(around(z + j, NZ), y, x, k))
    for j in range(1, NQ):
        greet(plane(around(q + j, NQ)))
    greet(to_sib)

    for load in loads:
        load.wait()

    col_blocks = omega_ref.shape[0]
    slots = vals_ref.shape[0]
    row_of, live, prods = [], [], []
    for b in range(slots):
        slot = slot_ref[0, b]
        on = count_ref[0, 0] > b
        row_of.append(lax.div(slot, col_blocks))
        live.append(jnp.where(on, 1.0, 0.0).astype(F32))
        picked = omega_ref[pl.ds(lax.rem(slot, col_blocks), 1)].reshape(BS, RANK)
        prods.append(jnp.dot(vals_ref[b], picked, preferred_element_type=F32))
        a_all[pl.ds(y, 1), b] = (vals_ref[b] * live[b].astype(jnp.bfloat16))[None]
        meta[pl.ds(y, 1), b] = jnp.full(
            (1,) + meta.shape[2:], jnp.where(on, lax.rem(slot, col_blocks), -1), jnp.int32
        )

    def fill(kk):
        for xx in range(NX):
            block = xx * NK + kk
            total = None
            for b in range(slots):
                term = prods[b] * (jnp.where(row_of[b] == block, 1.0, 0.0).astype(F32) * live[b])
                total = term if total is None else total + term
            part[pl.ds(kk, 1), xx] = total[None]

    fill(sib)
    pl.semaphore_wait(barrier, NQ + len(reach))
    for j in (3, -3):
        to = at(around(z + j, NZ), y, x, k)
        pl.semaphore_signal(beyond_sem, inc=1, device_id=to, device_id_type=MESH)

    def sib_copy(xx):
        return copy(part.at[sib, xx], r1.at[xx], r1_sem.at[xx], to_sib)

    half = BS // 2
    sides = (1, -1)

    def rows_of(i):
        return pl.ds(i * half, half)

    def relay_copy(i):
        src = part.at[k, around(x + 2, NX), rows_of(i)]
        return copy(src, relay.at[i], relay_sem.at[i], at(z, y, around(x + sides[i], NX), k))

    def x_copy(i, r):
        xx = around(x + sides[i], NX)
        src = part.at[k, xx, rows_of(r)]
        return copy(src, r2.at[i, rows_of(r)], r2_sem.at[i, r], at(z, y, xx, k))

    def a_copies(d):
        to = at(z, around(y + d, NY), x, k)
        return (
            copy(a_all.at[y], a_all.at[y], a_sem.at[d - 1], to),
            copy(meta.at[y], meta.at[y], m_sem.at[d - 1], to),
        )

    def join(d):
        xx = around(x + d, NX)
        sib_copy(xx).wait_recv()
        part[pl.ds(k, 1), pl.ds(xx, 1)] = (
            part[pl.ds(k, 1), pl.ds(xx, 1)] + r1[pl.ds(xx, 1)][None]
        )

    for d in (2, 1, 3, 0):
        go(sib_copy(around(x + d, NX)))
    fill(k)
    join(2)
    for i in range(2):
        go(relay_copy(i))
    for i in range(2):
        join(sides[i])
        go(x_copy(i, 1 - i))
    join(0)
    for i in range(2):
        relay_copy(i).wait_recv()
        at_rows = (pl.ds(k, 1), pl.ds(around(x + sides[i], NX), 1), rows_of(i))
        part[at_rows] = part[at_rows] + relay[i][None, None]
        go(x_copy(i, i))
    for i in range(2):
        for r in range(2):
            x_copy(i, r).wait_recv()
    own[...] = part[pl.ds(k, 1), pl.ds(x, 1)].reshape(BS, RANK) + r2[0] + r2[1]

    def gram_half(u, rows):
        pair = pairs[u]
        pair[pl.ds(k, 1)] = rows[None]
        go(copy(pair.at[k], pair.at[k], pair_sem.at[u], to_sib))
        copy(pair.at[k], pair.at[sib], pair_sem.at[u], to_sib).wait_recv()
        n = NK * rows.shape[0]
        lanes = pl.ds(pl.multiple_of(k * HALF, HALF), HALF)
        term = lax.dot_general(
            pair[:, :, lanes].reshape(n, HALF), pair[...].reshape(n, RANK), (((0,), (0,)), ((), ())),
            precision=HI, preferred_element_type=F32,
        )
        g_send[u] = term.reshape(NQ, PIECE, RANK)
        for j in range(1, NQ):
            qq = around(q + j, NQ)
            go(copy(g_send.at[u, qq], g_recv.at[u, q], g_sem.at[u], plane(qq)))
        g_recv[u, pl.ds(q, 1)] = g_send[u, pl.ds(q, 1)]

    def arrived(buffer, sem):
        copy(buffer, buffer, sem, to_sib).wait_recv()

    group, member = lax.div(z, NG), lax.rem(z, NG)
    way, reach0 = lax.div(member, 2) * 2 - 1, 4 - member * (3 - member)

    def reduce_plane(u):
        arrived(g_recv.at[u, pl.ds(0, NQ - 1)], g_sem.at[u])
        total = g_recv[u, 0]
        for i in range(1, NQ):
            total = total + g_recv[u, i]
        z_near[u, pl.ds(member, 1)] = total[None]
        mine = z_near.at[u, member]
        for j in range(1, NG):
            near = group * NG + around(member + j, NG)
            go(copy(mine, mine, near_sem.at[u], at(near, y, x, k)))

    def reduce_near(u):
        arrived(z_near.at[u, pl.ds(0, NG - 1)], near_sem.at[u])
        total = z_near[u, 0]
        for i in range(1, NG):
            total = total + z_near[u, i]
        z_far[u, pl.ds(group, 1)] = total[None]
        mine = z_far.at[u, group]
        if u == 0:
            pl.semaphore_wait(beyond_sem, 2)
        for j in (2, 1, 0):
            far = around(z + way * (reach0 + j), NZ)
            go(copy(mine, mine, far_sem.at[u], at(far, y, x, k)))

    def reduce_far(u):
        arrived(z_far.at[u, pl.ds(0, NZ // NG - 1)], far_sem.at[u])
        total = z_far[u, 0]
        for i in range(1, NZ // NG):
            total = total + z_far[u, i]
        g_all[u, pl.ds(k, 1), pl.ds(q, 1)] = total[None, None]
        mine = g_all.at[u, k, q]
        for j in range(1, NQ):
            go(copy(mine, mine, ag_sem.at[u], plane(around(q + j, NQ))))

    def gather_plane(u):
        flush()
        arrived(g_all.at[u, k, pl.ds(0, NQ - 1)], ag_sem.at[u])
        go(copy(g_all.at[u, k], g_all.at[u, k], half_sem.at[u], to_sib))
        copy(g_all.at[u, k], g_all.at[u, sib], half_sem.at[u], to_sib).wait_recv()
        return g_all[u].reshape(RANK, RANK)

    gram_half(0, own[...])

    parts = 2
    depth = BS // parts

    def s_copy(d, i):
        rows = pl.ds(i * depth, depth)
        return copy(
            own.at[rows], s_all.at[k, x, rows], s_sem.at[d - 1, i], at(z, y, around(x + d, NX), k)
        )

    def s_arrival(d, i):
        rows = pl.ds(i * depth, depth)
        return copy(
            own.at[rows], s_all.at[k, around(x - d, NX), rows], s_sem.at[d - 1, i], to_sib
        )

    def pick_copy(d):
        return copy(pick.at[y], pick.at[y], pick_sem.at[d - 1], at(z, around(y + d, NY), x, k))

    def pick_arrival(d):
        yy = around(y - d, NY)
        return copy(pick.at[y], pick.at[yy], pick_sem.at[d - 1], at(z, yy, x, k))

    s_all[pl.ds(k, 1), pl.ds(x, 1)] = own[...][None, None]
    reduce_plane(0)
    for d in (2, 1, 3):
        go(s_copy(d, 0))
    reduce_near(0)
    for d in (2, 1, 3):
        go(s_copy(d, 1))
    for d in (2, 1, 3):
        for c in a_copies(d):
            go(c)
    reduce_far(0)
    for d in (1, 3, 2):
        for i in range(parts):
            s_arrival(d, i).wait_recv()
    go(copy(s_all.at[k], s_all.at[k], sib_sem, to_sib))
    copy(s_all.at[k], s_all.at[sib], sib_sem, to_sib).wait_recv()
    for b in range(slots):
        rows = s_all[pl.ds(lax.rem(row_of[b], NK), 1), pl.ds(lax.div(row_of[b], NK), 1)]
        pick[pl.ds(y, 1), b] = rows.reshape(1, BS, RANK)
    gram[...] = gather_plane(0) * (1.0 / (BS * RB * NY * NZ))

    for d in (1, 3):
        go(pick_copy(d))
    inverse_factor(gram, linv)

    def split(v):
        high = v.astype(jnp.bfloat16)
        rest = v - high.astype(F32)
        middle = rest.astype(jnp.bfloat16)
        return high, middle, (rest - middle.astype(F32)).astype(jnp.bfloat16)

    high, middle, low = split(linv[...].T)
    for i, v in enumerate((high, high, high, middle, middle, low)):
        factor[pl.ds(i * RANK, RANK), :] = v

    def basis_rows(rows):
        high, middle, low = split(rows)
        wide = jnp.concatenate([high, middle, low, high, middle, high], axis=1)
        return jnp.dot(wide, factor[...], preferred_element_type=F32).astype(jnp.bfloat16)

    before, after, across = around(y - 1, NY), around(y + 1, NY), around(y + 2, NY)
    part0, part1 = pl.ds(0, slots // 2), pl.ds(slots // 2, slots - slots // 2)

    def pass_on(i, yy):
        blocks = (part0, part1)[i]
        to = at(z, (after, before)[i], x, k)
        return copy(ready.at[yy, blocks], ready.at[yy, blocks], ready_sem.at[i], to)

    def form(*which):
        rows = basis_rows(
            jnp.concatenate([pick[pl.ds(yy, 1), b].reshape(b.size * BS, RANK) for yy, b in which])
        )
        at_row = 0
        for yy, b in which:
            ready[pl.ds(yy, 1), b] = rows[at_row : at_row + b.size * BS].reshape(
                1, b.size, BS, RANK
            )
            at_row += b.size * BS

    for d in (1, 3):
        pick_arrival(d).wait_recv()
    form((before, part0), (after, part1))
    go(pass_on(0, before))
    go(pass_on(1, after))
    form((y, pl.ds(0, slots)))
    form((before, part1), (after, part0))
    basis_ref[...] = basis_rows(own[...])

    def products(yy):
        def one(b, carry):
            prod[pl.ds(yy, 1), pl.ds(b, 1)] = lax.dot_general(
                a_all[pl.ds(yy, 1), pl.ds(b, 1)].reshape(BS, BS),
                ready[pl.ds(yy, 1), pl.ds(b, 1)].reshape(BS, RANK),
                (((0,), (0,)), ((), ())), preferred_element_type=F32,
            )[None, None]
            return carry

        lax.fori_loop(0, slots, one, 0)

    products(y)
    for d in (1, 3, 2):
        yy = around(y - d, NY)
        to = at(z, yy, x, k)
        copy(a_all.at[y], a_all.at[yy], a_sem.at[d - 1], to).wait_recv()
        copy(meta.at[y], meta.at[yy], m_sem.at[d - 1], to).wait_recv()
        if d == 2:
            pass_on(0, across).wait_recv()
            pass_on(1, across).wait_recv()
        products(yy)

    tile = 16
    per_strip = STRIP // tile

    def coded(v):
        top = jnp.maximum(jnp.max(jnp.abs(v), axis=0, keepdims=True), 1e-33)
        return jnp.round(v * (STEPS / top)).astype(jnp.int32).astype(jnp.int16), top * (1.0 / STEPS)

    def value(steps, unit):
        return steps.astype(jnp.int32).astype(F32) * unit

    def place(zz, carry):
        totals = []
        for t in range(per_strip):
            g = zz * (NY * per_strip) + y * per_strip + t
            block = lax.div(g, BS // tile)
            rows = pl.multiple_of(lax.rem(g, BS // tile) * tile, tile)
            total = jnp.zeros((tile, RANK), F32)
            for yy in range(NY):
                for b in range(slots):
                    here = jnp.concatenate([meta[yy, b] == block] * (RANK // 128), axis=1)
                    total = total + jnp.where(here, prod[yy, b, pl.ds(rows, tile), :], 0.0)
            totals.append(total)
        total = jnp.concatenate(totals, axis=0)
        strip[pl.ds(zz, 1)] = total[None]
        steps, unit = coded(total)
        code1[pl.ds(zz, 1)] = steps[None]
        unit1[pl.ds(zz, 1)] = unit[None]
        return carry


    sign = 1 - 2 * k
    near = (1, -1, 2)

    def w1_copy(i, e):
        mid = around(z + sign * near[i], NZ)
        dest = around(mid + FAR[e], NZ)
        return copy(code1.at[dest], w1.at[e, i], w1_sem.at[e, i], at(mid, y, x, k))

    def c1_copy(i, e):
        mid = around(z + sign * near[i], NZ)
        dest = around(mid + FAR[e], NZ)
        return copy(unit1.at[dest], c1.at[e, i], c1_sem.at[e, i], at(mid, y, x, k))

    def w2_copies(e):
        to = at(around(z + FAR[e], NZ), y, x, k)
        return (
            copy(code2.at[e], w2.at[e], w2_sem.at[e], to),
            copy(unit2.at[e], c2.at[e], c2_sem.at[e], to),
        )

    for e in range(4):

        def put(i, carry):
            step = jnp.where(i == 3, 0, jnp.where(i == 2, 2, 1 - 2 * i))
            return place(around(around(z + sign * step, NZ) + FAR[e], NZ), carry)

        lax.fori_loop(0, 4, put, 0)
        for i in (2, 0, 1):
            go(w1_copy(i, e))
            go(c1_copy(i, e))
    for e in range(4):
        dest = around(z + FAR[e], NZ)
        total = strip[pl.ds(dest, 1)].reshape(STRIP, RANK)
        for i in range(3):
            w1_copy(i, e).wait_recv()
            c1_copy(i, e).wait_recv()
            total = total + value(w1[e, i], c1[e, i])
        code2[e], unit2[e] = coded(total)
        for c in w2_copies(e):
            go(c)
    proj = jnp.zeros((STRIP, RANK), F32)
    for e in range(4):
        for c in w2_copies(e):
            c.wait_recv()
        proj = proj + value(w2[e], c2[e])
    proj = proj * (1.0 / 256.0)
    proj_ref[0] = proj

    gram_half(1, proj)
    reduce_plane(1)
    reduce_near(1)
    reduce_far(1)
    core_ref[...] = gather_plane(1) / float(col_blocks * BS * NX * NK)

    flush()


def body(block_vals, block_slot, block_count, omega):
    slots = block_vals.shape[0]
    vmem = pl.BlockSpec(memory_space=pltpu.VMEM)
    hbm = pl.BlockSpec(memory_space=pltpu.HBM)
    dma = pltpu.SemaphoreType.DMA
    blocks = lambda *lead: pltpu.VMEM((*lead, BS, RANK), F32)
    inputs = [
        pltpu.with_memory_space_constraint(a, pltpu.HBM)
        for a in (block_vals, block_slot.T, omega.reshape(-1, BS, RANK))
    ]
    basis, projected, core = pl.pallas_call(
        kernel,
        out_shape=(
            pltpu.VMEM((BS, RANK), jnp.bfloat16),
            pltpu.VMEM((1, STRIP, RANK), F32),
            pltpu.VMEM((RANK, RANK), F32),
        ),
        in_specs=[hbm] * 3 + [pl.BlockSpec(memory_space=pltpu.SMEM)],
        out_specs=(vmem, vmem, vmem),
        scratch_shapes=[
            pltpu.VMEM(block_vals.shape, block_vals.dtype),
            pltpu.SMEM(block_slot.shape[::-1], jnp.int32),
            pltpu.VMEM((omega.shape[0] // BS, BS, RANK), omega.dtype),
            blocks(NK, NX),
            blocks(NX),
            pltpu.VMEM((2, BS // 2, RANK), F32),
            blocks(2),
            blocks(),
            blocks(NK, NX),
            blocks(NY, slots),
            pltpu.VMEM((NY, slots, BS, RANK), jnp.bfloat16),
            pltpu.VMEM((NY, slots, BS, BS), jnp.bfloat16),
            pltpu.VMEM((NY, slots, 16, 128), jnp.int32),
            blocks(NK),
            pltpu.VMEM((NK, STRIP, RANK), F32),
            pltpu.VMEM((2, NQ, PIECE, RANK), F32),
            pltpu.VMEM((2, NQ, PIECE, RANK), F32),
            pltpu.VMEM((2, NG, PIECE, RANK), F32),
            pltpu.VMEM((2, NZ // NG, PIECE, RANK), F32),
            pltpu.VMEM((2, NK, NQ, PIECE, RANK), F32),
            pltpu.VMEM((RANK, RANK), F32),
            pltpu.VMEM((RANK, RANK), F32),
            pltpu.VMEM((6 * RANK, RANK), jnp.bfloat16),
            blocks(NY, slots),
            pltpu.VMEM((NZ, STRIP, RANK), F32),
            pltpu.VMEM((NZ, STRIP, RANK), jnp.int16),
            pltpu.VMEM((NZ, 1, RANK), F32),
            pltpu.VMEM((4, STRIP, RANK), jnp.int16),
            pltpu.VMEM((4, 1, RANK), F32),
            pltpu.VMEM((4, 3, STRIP, RANK), jnp.int16),
            pltpu.VMEM((4, 3, 1, RANK), F32),
            pltpu.VMEM((4, STRIP, RANK), jnp.int16),
            pltpu.VMEM((4, 1, RANK), F32),
            pltpu.SemaphoreType.REGULAR,
            dma((3,)), dma,
            dma((NX,)), dma((2,)), dma((2, 2)), dma((NX - 1, 2)), dma, dma((NY - 1,)), dma((NY - 1,)), dma((NY - 1,)), dma((2,)),
            dma((2,)), dma((2,)), dma((2,)), dma((2,)), dma((2,)), dma((2,)), dma((4, 3)), dma((4, 3)), dma((4,)), dma((4,)),
        ],
        compiler_params=pltpu.CompilerParams(
            collective_id=0, has_side_effects=True, vmem_limit_bytes=60 * 2**20
        ),
        name="range_basis",
    )(*inputs, block_count)
    return basis, projected, core


def solution(mesh):
    placed = (P("row", "col", None), P("row", "col"), P("row", "col"), P("col", None))
    return jax.shard_map(
        body,
        mesh=mesh,
        in_specs=placed,
        out_specs=(P(("row", "col"), None), P("col", "row", None), P()),
        check_vma=False,
    )
```

```python
import functools

import jax
import jax.numpy as jnp
from jax import lax
from jax.experimental import pallas as pl
from jax.experimental.pallas import tpu as pltpu
from jax.sharding import PartitionSpec as P

MESH = pl.DeviceIdType.MESH
HI = lax.Precision.HIGHEST
F32 = jnp.float32

RB = 8
BS = 128
RANK = 256
NY, NZ, NX, NK = 4, 16, 4, 2
NQ = NY * NX
HALF = RANK // NK
PIECE = HALF // NQ
STRIP = 48
PB, SB = 64, 16
NG = 4
STEPS = 32767.0
FAR = (6, -6, 2, -2)


def split(v):
    high = v.astype(jnp.bfloat16)
    rest = v - high.astype(F32)
    middle = rest.astype(jnp.bfloat16)
    return high, middle, (rest - middle.astype(F32)).astype(jnp.bfloat16)


def inverse_factor(a_ref, out_ref):
    n = a_ref.shape[0]
    lane = lax.broadcasted_iota(jnp.int32, (PB, n), 1)
    lane8 = lax.broadcasted_iota(jnp.int32, (8, 128), 1)
    sub8 = lax.broadcasted_iota(jnp.int32, (8, 128), 0)
    lane_rest = lax.broadcasted_iota(jnp.int32, (n - PB, n), 1)
    tiles, halves = PB // 8, n // 128

    def wide(v, i):
        return jnp.broadcast_to(v[i : i + 1], (8, 128))

    def panel(p, carry):
        w = [
            [a_ref[8 * t : 8 * t + 8, 128 * h : 128 * h + 128] for h in range(halves)]
            for t in range(tiles)
        ]
        for base in range(0, PB, SB):
            first, last = base // 8, (base + SB) // 8
            cols = [
                {
                    t: jnp.broadcast_to(w[t][0][:, base + j : base + j + 1], (8, 128))
                    for t in range(first, tiles)
                }
                for j in range(SB)
            ]
            inside = (lane8 >= base) & (lane8 < base + SB)
            for t in range(tiles):
                fresh = jnp.where(lane8 == sub8 + 8 * t, 1.0, 0.0) if first <= t < last else 0.0
                w[t][0] = jnp.where(inside, fresh, w[t][0])
            for k in range(SB):
                tk, sk = divmod(base + k, 8)
                r = lax.rsqrt(wide(cols[k][tk], sk))
                m = {t: cols[k][t] * r for t in range(tk, tiles)}
                m[tk] = jnp.where(sub8 > sk, m[tk], 0.0)
                for j in range(k + 1, SB):
                    c = wide(cols[j][tk], sk) * r
                    for t in range(tk, tiles):
                        cols[j][t] = cols[j][t] - m[t] * c
                for h in range(halves):
                    u = wide(w[tk][h], sk) * r
                    for t in range(tk, tiles):
                        w[t][h] = w[t][h] - m[t] * u
                    w[tk][h] = jnp.where(sub8 == sk, u, w[tk][h])
        done = jnp.concatenate([jnp.concatenate(r, axis=1) for r in w], axis=0)
        placed = pltpu.roll(done, p * PB, 1)
        out_ref[pl.ds(pl.multiple_of(p * PB, PB), PB), :] = jnp.where(
            lane < (p + 1) * PB, placed, 0.0
        )

        @pl.when(p < n // PB - 1)
        def _():
            turned = pltpu.roll(done, n - PB, 1)
            rest = pltpu.roll(jnp.where(lane_rest < PB, 0.0, a_ref[PB:n, :]), n - PB, 1)
            high, middle, low = split(turned)
            step = lax.dot_general(
                jnp.concatenate([high, middle, low, high, middle, high], axis=0),
                jnp.concatenate([high, high, high, middle, middle, low], axis=0),
                (((0,), (0,)), ((), ())), preferred_element_type=F32,
            )
            a_ref[0 : n - PB, :] = rest - step[0 : n - PB]

        return carry

    lax.fori_loop(0, n // PB, panel, 0)


def kernel(
    vals_hbm, slot_hbm, omega_hbm, count_ref,
    basis_ref, proj_ref, core_ref,
    vals_ref, slot_ref, omega_ref,
    part, r1, relay, r2, own, s_all, pick, ready, a_all, meta,
    pair0, pair1, g_send, g_recv, z_near, z_far, g_all,
    gram, linv, factor, prod, strip, code1, unit1, code2, unit2, w1, c1, w2, c2,
    beyond_sem, load_sem, send_sem, r1_sem, relay_sem, r2_sem, s_sem, sib_sem, a_sem, m_sem, pick_sem, ready_sem,
    pair_sem, g_sem, near_sem, far_sem, ag_sem, half_sem, w1_sem, c1_sem, w2_sem, c2_sem,
):
    row, col = lax.axis_index("row"), lax.axis_index("col")
    z, y = lax.div(row, NY), lax.rem(row, NY)
    x, k = lax.div(col, NK), lax.rem(col, NK)
    sib = 1 - k
    q = y * NX + x
    pending = []
    pairs = (pair0, pair1)

    def around(i, n):
        return lax.rem(i + n, n)

    def at(zz, yy, xx, kk):
        return (zz * NY + yy, xx * NK + kk)

    def plane(qq):
        return at(z, lax.div(qq, NX), lax.rem(qq, NX), k)

    to_sib = at(z, y, x, sib)

    def copy(src, dst, recv_sem, device):
        return pltpu.make_async_remote_copy(
            src_ref=src, dst_ref=dst, send_sem=send_sem, recv_sem=recv_sem,
            device_id=device, device_id_type=MESH,
        )

    def go(c):
        c.start()
        pending.append(c.wait_send)

    def flush():
        while pending:
            pending.pop(0)()

    moves = ((slot_hbm, slot_ref), (vals_hbm, vals_ref), (omega_hbm, omega_ref))
    loads = [pltpu.make_async_copy(a, b, load_sem.at[i]) for i, (a, b) in enumerate(moves)]
    for load in loads:
        load.start()

    barrier = pltpu.get_barrier_semaphore()

    def greet(device):
        pl.semaphore_signal(barrier, inc=1, device_id=device, device_id_type=MESH)

    reach = (3, -3, 2, -2, 1, -1)
    for j in reach:
        greet(at(around(z + j, NZ), y, x, k))
    for j in range(1, NQ):
        greet(plane(around(q + j, NQ)))
    greet(to_sib)

    for load in loads:
        load.wait()

    col_blocks = omega_ref.shape[0]
    slots = vals_ref.shape[0]
    row_of, column, live, prods = [], [], [], []
    for b in range(slots):
        slot = slot_ref[0, b]
        on = count_ref[0, 0] > b
        row_of.append(lax.div(slot, col_blocks))
        live.append(jnp.where(on, 1.0, 0.0).astype(F32))
        picked = omega_ref[pl.ds(lax.rem(slot, col_blocks), 1)].reshape(BS, RANK)
        prods.append(jnp.dot(vals_ref[b], picked, preferred_element_type=F32))
        column.append(jnp.where(on, lax.rem(slot, col_blocks), -1))

    def fill(kk, xx):
        total = None
        for b in range(slots):
            here = row_of[b] == xx * NK + kk
            term = prods[b] * (jnp.where(here, 1.0, 0.0).astype(F32) * live[b])
            total = term if total is None else total + term
        part[pl.ds(kk, 1), pl.ds(xx, 1)] = total[None, None]

    pl.semaphore_wait(barrier, NQ + len(reach))
    for j in (3, -3):
        to = at(around(z + j, NZ), y, x, k)
        pl.semaphore_signal(beyond_sem, inc=1, device_id=to, device_id_type=MESH)

    def sib_copy(xx):
        return copy(part.at[sib, xx], r1.at[xx], r1_sem.at[xx], to_sib)

    half = BS // 2
    sides = (1, -1)

    def rows_of(i):
        return pl.ds(i * half, half)

    def relay_copy(i):
        src = part.at[k, around(x + 2, NX), rows_of(i)]
        return copy(src, relay.at[i], relay_sem.at[i], at(z, y, around(x + sides[i], NX), k))

    def x_copy(i, r):
        xx = around(x + sides[i], NX)
        src = part.at[k, xx, rows_of(r)]
        return copy(src, r2.at[i, rows_of(r)], r2_sem.at[i, r], at(z, y, xx, k))

    def a_copies(d):
        to = at(z, around(y + d, NY), x, k)
        return (
            copy(a_all.at[y], a_all.at[y], a_sem.at[d - 1], to),
            copy(meta.at[y], meta.at[y], m_sem.at[d - 1], to),
        )

    def join(d):
        xx = around(x + d, NX)
        sib_copy(xx).wait_recv()
        part[pl.ds(k, 1), pl.ds(xx, 1)] = (
            part[pl.ds(k, 1), pl.ds(xx, 1)] + r1[pl.ds(xx, 1)][None]
        )

    for d in (2, 1, 3, 0):
        xx = around(x + d, NX)
        fill(sib, xx)
        go(sib_copy(xx))
    for xx in range(NX):
        fill(k, xx)
    for b in range(slots):
        a_all[pl.ds(y, 1), b] = (vals_ref[b] * live[b].astype(jnp.bfloat16))[None]
        meta[pl.ds(y, 1), b] = jnp.full((1,) + meta.shape[2:], column[b], jnp.int32)
    join(2)
    for i in range(2):
        go(relay_copy(i))
    for i in range(2):
        join(sides[i])
        go(x_copy(i, 1 - i))
    join(0)
    for i in range(2):
        relay_copy(i).wait_recv()
        at_rows = (pl.ds(k, 1), pl.ds(around(x + sides[i], NX), 1), rows_of(i))
        part[at_rows] = part[at_rows] + relay[i][None, None]
        go(x_copy(i, i))
    for i in range(2):
        for r in range(2):
            x_copy(i, r).wait_recv()
    own[...] = part[pl.ds(k, 1), pl.ds(x, 1)].reshape(BS, RANK) + r2[0] + r2[1]

    def gram_half(u, rows):
        pair = pairs[u]
        pair[pl.ds(k, 1)] = rows[None]
        go(copy(pair.at[k], pair.at[k], pair_sem.at[u], to_sib))
        copy(pair.at[k], pair.at[sib], pair_sem.at[u], to_sib).wait_recv()
        n = NK * rows.shape[0]
        lanes = pl.ds(pl.multiple_of(k * HALF, HALF), HALF)
        term = lax.dot_general(
            pair[:, :, lanes].reshape(n, HALF), pair[...].reshape(n, RANK), (((0,), (0,)), ((), ())),
            precision=HI, preferred_element_type=F32,
        )
        g_send[u] = term.reshape(NQ, PIECE, RANK)
        for j in range(1, NQ):
            qq = around(q + j, NQ)
            go(copy(g_send.at[u, qq], g_recv.at[u, q], g_sem.at[u], plane(qq)))
        g_recv[u, pl.ds(q, 1)] = g_send[u, pl.ds(q, 1)]

    def arrived(buffer, sem):
        copy(buffer, buffer, sem, to_sib).wait_recv()

    group, member = lax.div(z, NG), lax.rem(z, NG)
    way, reach0 = lax.div(member, 2) * 2 - 1, 4 - member * (3 - member)

    def reduce_plane(u):
        arrived(g_recv.at[u, pl.ds(0, NQ - 1)], g_sem.at[u])
        total = g_recv[u, 0]
        for i in range(1, NQ):
            total = total + g_recv[u, i]
        z_near[u, pl.ds(member, 1)] = total[None]
        mine = z_near.at[u, member]
        for j in range(1, NG):
            near = group * NG + around(member + j, NG)
            go(copy(mine, mine, near_sem.at[u], at(near, y, x, k)))

    def reduce_near(u):
        arrived(z_near.at[u, pl.ds(0, NG - 1)], near_sem.at[u])
        total = z_near[u, 0]
        for i in range(1, NG):
            total = total + z_near[u, i]
        z_far[u, pl.ds(group, 1)] = total[None]
        mine = z_far.at[u, group]
        if u == 0:
            pl.semaphore_wait(beyond_sem, 2)
        for j in (2, 1, 0):
            far = around(z + way * (reach0 + j), NZ)
            go(copy(mine, mine, far_sem.at[u], at(far, y, x, k)))

    def reduce_far(u):
        arrived(z_far.at[u, pl.ds(0, NZ // NG - 1)], far_sem.at[u])
        total = z_far[u, 0]
        for i in range(1, NZ // NG):
            total = total + z_far[u, i]
        total = total * (1.0 / (BS * RB * NY * NZ) if u == 0 else 1.0 / (col_blocks * BS * NX * NK))
        g_all[u, pl.ds(k, 1), pl.ds(q, 1)] = total[None, None]
        mine = g_all.at[u, k, q]
        for j in range(1, NQ):
            go(copy(mine, mine, ag_sem.at[u], plane(around(q + j, NQ))))

    def gather_plane(u):
        flush()
        arrived(g_all.at[u, k, pl.ds(0, NQ - 1)], ag_sem.at[u])
        go(copy(g_all.at[u, k], g_all.at[u, k], half_sem.at[u], to_sib))
        copy(g_all.at[u, k], g_all.at[u, sib], half_sem.at[u], to_sib).wait_recv()
        return g_all[u].reshape(RANK, RANK)

    gram_half(0, own[...])

    parts = 2
    depth = BS // parts

    def s_copy(d, i):
        rows = pl.ds(i * depth, depth)
        return copy(
            own.at[rows], s_all.at[k, x, rows], s_sem.at[d - 1, i], at(z, y, around(x + d, NX), k)
        )

    def s_arrival(d, i):
        rows = pl.ds(i * depth, depth)
        return copy(
            own.at[rows], s_all.at[k, around(x - d, NX), rows], s_sem.at[d - 1, i], to_sib
        )

    def pick_copy(d):
        return copy(pick.at[y], pick.at[y], pick_sem.at[d - 1], at(z, around(y + d, NY), x, k))

    def pick_arrival(d):
        yy = around(y - d, NY)
        return copy(pick.at[y], pick.at[yy], pick_sem.at[d - 1], at(z, yy, x, k))

    s_all[pl.ds(k, 1), pl.ds(x, 1)] = own[...][None, None]
    reduce_plane(0)
    for d in (2, 1, 3):
        go(s_copy(d, 0))
    reduce_near(0)
    for d in (2, 1, 3):
        go(s_copy(d, 1))
    for d in (2, 1, 3):
        for c in a_copies(d):
            go(c)
    reduce_far(0)
    for d in (1, 3, 2):
        for i in range(parts):
            s_arrival(d, i).wait_recv()
    go(copy(s_all.at[k], s_all.at[k], sib_sem, to_sib))
    copy(s_all.at[k], s_all.at[sib], sib_sem, to_sib).wait_recv()
    for b in range(slots):
        rows = s_all[pl.ds(lax.rem(row_of[b], NK), 1), pl.ds(lax.div(row_of[b], NK), 1)]
        pick[pl.ds(y, 1), b] = rows.reshape(1, BS, RANK)
    gram[...] = gather_plane(0)

    for d in (1, 3):
        go(pick_copy(d))
    inverse_factor(gram, linv)

    high, middle, low = split(linv[...].T)
    for i, v in enumerate((high, high, high, middle, middle, low)):
        factor[pl.ds(i * RANK, RANK), :] = v

    def basis_rows(rows):
        high, middle, low = split(rows)
        wide = jnp.concatenate([high, middle, low, high, middle, high], axis=1)
        return jnp.dot(wide, factor[...], preferred_element_type=F32).astype(jnp.bfloat16)

    before, after, across = around(y - 1, NY), around(y + 1, NY), around(y + 2, NY)
    part0, part1 = pl.ds(0, slots // 2), pl.ds(slots // 2, slots - slots // 2)

    def pass_on(i, yy):
        blocks = (part0, part1)[i]
        to = at(z, (after, before)[i], x, k)
        return copy(ready.at[yy, blocks], ready.at[yy, blocks], ready_sem.at[i], to)

    def form(*which):
        rows = basis_rows(
            jnp.concatenate([pick[pl.ds(yy, 1), b].reshape(b.size * BS, RANK) for yy, b in which])
        )
        at_row = 0
        for yy, b in which:
            ready[pl.ds(yy, 1), b] = rows[at_row : at_row + b.size * BS].reshape(
                1, b.size, BS, RANK
            )
            at_row += b.size * BS

    for d in (1, 3):
        pick_arrival(d).wait_recv()
    form((before, part0), (after, part1))
    go(pass_on(0, before))
    go(pass_on(1, after))
    form((y, pl.ds(0, slots)))
    form((before, part1), (after, part0))
    basis_ref[...] = basis_rows(own[...])

    def products(yy):
        def one(b, carry):
            prod[pl.ds(yy, 1), pl.ds(b, 1)] = lax.dot_general(
                a_all[pl.ds(yy, 1), pl.ds(b, 1)].reshape(BS, BS),
                ready[pl.ds(yy, 1), pl.ds(b, 1)].reshape(BS, RANK),
                (((0,), (0,)), ((), ())), preferred_element_type=F32,
            )[None, None]
            return carry

        lax.fori_loop(0, slots, one, 0)

    products(y)
    for d in (1, 3, 2):
        yy = around(y - d, NY)
        to = at(z, yy, x, k)
        copy(a_all.at[y], a_all.at[yy], a_sem.at[d - 1], to).wait_recv()
        copy(meta.at[y], meta.at[yy], m_sem.at[d - 1], to).wait_recv()
        if d == 2:
            pass_on(0, across).wait_recv()
            pass_on(1, across).wait_recv()
        products(yy)

    tile = 16
    per_strip = STRIP // tile

    def coded(v):
        top = jnp.maximum(jnp.max(jnp.abs(v), axis=0, keepdims=True), 1e-33)
        return jnp.round(v * (STEPS / top)).astype(jnp.int32).astype(jnp.int16), top * (1.0 / STEPS)

    def value(steps, unit):
        return steps.astype(jnp.int32).astype(F32) * unit

    def place(zz, carry):
        totals = []
        for t in range(per_strip):
            g = zz * (NY * per_strip) + y * per_strip + t
            block = lax.div(g, BS // tile)
            rows = pl.multiple_of(lax.rem(g, BS // tile) * tile, tile)
            total = jnp.zeros((tile, RANK), F32)
            for yy in range(NY):
                for b in range(slots):
                    here = jnp.concatenate([meta[yy, b] == block] * (RANK // 128), axis=1)
                    total = total + jnp.where(here, prod[yy, b, pl.ds(rows, tile), :], 0.0)
            totals.append(total)
        total = jnp.concatenate(totals, axis=0)
        strip[pl.ds(zz, 1)] = total[None]
        steps, unit = coded(total)
        code1[pl.ds(zz, 1)] = steps[None]
        unit1[pl.ds(zz, 1)] = unit[None]
        return carry


    sign = 1 - 2 * k
    near = (1, -1, 2)

    def w1_copy(i, e):
        mid = around(z + sign * near[i], NZ)
        dest = around(mid + FAR[e], NZ)
        return copy(code1.at[dest], w1.at[e, i], w1_sem.at[e, i], at(mid, y, x, k))

    def c1_copy(i, e):
        mid = around(z + sign * near[i], NZ)
        dest = around(mid + FAR[e], NZ)
        return copy(unit1.at[dest], c1.at[e, i], c1_sem.at[e, i], at(mid, y, x, k))

    def w2_copies(e):
        to = at(around(z + FAR[e], NZ), y, x, k)
        return (
            copy(code2.at[e], w2.at[e], w2_sem.at[e], to),
            copy(unit2.at[e], c2.at[e], c2_sem.at[e], to),
        )

    for e in range(4):

        def put(i, carry):
            step = jnp.where(i == 3, 0, jnp.where(i == 2, 2, 1 - 2 * i))
            return place(around(around(z + sign * step, NZ) + FAR[e], NZ), carry)

        lax.fori_loop(0, 4, put, 0)
        for i in (2, 0, 1):
            go(w1_copy(i, e))
            go(c1_copy(i, e))
    for e in range(4):
        dest = around(z + FAR[e], NZ)
        total = strip[pl.ds(dest, 1)].reshape(STRIP, RANK)
        for i in range(3):
            w1_copy(i, e).wait_recv()
            c1_copy(i, e).wait_recv()
            total = total + value(w1[e, i], c1[e, i])
        code2[e], unit2[e] = coded(total)
        for c in w2_copies(e):
            go(c)
    proj = jnp.zeros((STRIP, RANK), F32)
    for e in range(4):
        for c in w2_copies(e):
            c.wait_recv()
        proj = proj + value(w2[e], c2[e])
    proj = proj * (1.0 / 256.0)
    proj_ref[0] = proj

    gram_half(1, proj)
    reduce_plane(1)
    reduce_near(1)
    reduce_far(1)
    core_ref[...] = gather_plane(1)

    flush()


def body(block_vals, block_slot, block_count, omega):
    slots = block_vals.shape[0]
    vmem = pl.BlockSpec(memory_space=pltpu.VMEM)
    hbm = pl.BlockSpec(memory_space=pltpu.HBM)
    dma = pltpu.SemaphoreType.DMA
    blocks = lambda *lead: pltpu.VMEM((*lead, BS, RANK), F32)
    inputs = [
        pltpu.with_memory_space_constraint(a, pltpu.HBM)
        for a in (block_vals, block_slot.T, omega.reshape(-1, BS, RANK))
    ]
    basis, projected, core = pl.pallas_call(
        kernel,
        out_shape=(
            pltpu.VMEM((BS, RANK), jnp.bfloat16),
            pltpu.VMEM((1, STRIP, RANK), F32),
            pltpu.VMEM((RANK, RANK), F32),
        ),
        in_specs=[hbm] * 3 + [pl.BlockSpec(memory_space=pltpu.SMEM)],
        out_specs=(vmem, vmem, vmem),
        scratch_shapes=[
            pltpu.VMEM(block_vals.shape, block_vals.dtype),
            pltpu.SMEM(block_slot.shape[::-1], jnp.int32),
            pltpu.VMEM((omega.shape[0] // BS, BS, RANK), omega.dtype),
            blocks(NK, NX),
            blocks(NX),
            pltpu.VMEM((2, BS // 2, RANK), F32),
            blocks(2),
            blocks(),
            blocks(NK, NX),
            blocks(NY, slots),
            pltpu.VMEM((NY, slots, BS, RANK), jnp.bfloat16),
            pltpu.VMEM((NY, slots, BS, BS), jnp.bfloat16),
            pltpu.VMEM((NY, slots, 16, 128), jnp.int32),
            blocks(NK),
            pltpu.VMEM((NK, STRIP, RANK), F32),
            pltpu.VMEM((2, NQ, PIECE, RANK), F32),
            pltpu.VMEM((2, NQ, PIECE, RANK), F32),
            pltpu.VMEM((2, NG, PIECE, RANK), F32),
            pltpu.VMEM((2, NZ // NG, PIECE, RANK), F32),
            pltpu.VMEM((2, NK, NQ, PIECE, RANK), F32),
            pltpu.VMEM((RANK, RANK), F32),
            pltpu.VMEM((RANK, RANK), F32),
            pltpu.VMEM((6 * RANK, RANK), jnp.bfloat16),
            blocks(NY, slots),
            pltpu.VMEM((NZ, STRIP, RANK), F32),
            pltpu.VMEM((NZ, STRIP, RANK), jnp.int16),
            pltpu.VMEM((NZ, 1, RANK), F32),
            pltpu.VMEM((4, STRIP, RANK), jnp.int16),
            pltpu.VMEM((4, 1, RANK), F32),
            pltpu.VMEM((4, 3, STRIP, RANK), jnp.int16),
            pltpu.VMEM((4, 3, 1, RANK), F32),
            pltpu.VMEM((4, STRIP, RANK), jnp.int16),
            pltpu.VMEM((4, 1, RANK), F32),
            pltpu.SemaphoreType.REGULAR,
            dma((3,)), dma,
            dma((NX,)), dma((2,)), dma((2, 2)), dma((NX - 1, 2)), dma, dma((NY - 1,)), dma((NY - 1,)), dma((NY - 1,)), dma((2,)),
            dma((2,)), dma((2,)), dma((2,)), dma((2,)), dma((2,)), dma((2,)), dma((4, 3)), dma((4, 3)), dma((4,)), dma((4,)),
        ],
        compiler_params=pltpu.CompilerParams(
            collective_id=0, has_side_effects=True, vmem_limit_bytes=60 * 2**20
        ),
        name="range_basis",
    )(*inputs, block_count)
    return basis, projected, core


def solution(mesh):
    placed = (P("row", "col", None), P("row", "col"), P("row", "col"), P("col", None))
    return jax.shard_map(
        body,
        mesh=mesh,
        in_specs=placed,
        out_specs=(P(("row", "col"), None), P("col", "row", None), P()),
        check_vma=False,
    )
```

```python
import functools

import jax
import jax.numpy as jnp
from jax import lax
from jax.experimental import pallas as pl
from jax.experimental.pallas import tpu as pltpu
from jax.sharding import PartitionSpec as P

MESH = pl.DeviceIdType.MESH
HI = lax.Precision.HIGHEST
F32 = jnp.float32

RB = 8
BS = 128
RANK = 256
NY, NZ, NX, NK = 4, 16, 4, 2
NQ = NY * NX
HALF = RANK // NK
PIECE = HALF // NQ
STRIP = 48
PB, SB = 64, 16
NG = 4
STEPS = 32767.0
FAR = (6, -6, 2, -2)


def split(v):
    high = v.astype(jnp.bfloat16)
    rest = v - high.astype(F32)
    middle = rest.astype(jnp.bfloat16)
    return high, middle, (rest - middle.astype(F32)).astype(jnp.bfloat16)


def inverse_factor(a_ref, out_ref):
    n = a_ref.shape[0]
    lane = lax.broadcasted_iota(jnp.int32, (PB, n), 1)
    lane8 = lax.broadcasted_iota(jnp.int32, (8, 128), 1)
    sub8 = lax.broadcasted_iota(jnp.int32, (8, 128), 0)
    lane_rest = lax.broadcasted_iota(jnp.int32, (n - PB, n), 1)
    tiles, halves = PB // 8, n // 128

    def wide(v, i):
        return jnp.broadcast_to(v[i : i + 1], (8, 128))

    def panel(p, carry):
        w = [
            [a_ref[8 * t : 8 * t + 8, 128 * h : 128 * h + 128] for h in range(halves)]
            for t in range(tiles)
        ]
        for base in range(0, PB, SB):
            first, last = base // 8, (base + SB) // 8
            cols = [
                {
                    t: jnp.broadcast_to(w[t][0][:, base + j : base + j + 1], (8, 128))
                    for t in range(first, tiles)
                }
                for j in range(SB)
            ]
            inside = (lane8 >= base) & (lane8 < base + SB)
            for t in range(tiles):
                fresh = jnp.where(lane8 == sub8 + 8 * t, 1.0, 0.0) if first <= t < last else 0.0
                w[t][0] = jnp.where(inside, fresh, w[t][0])
            for k in range(SB):
                tk, sk = divmod(base + k, 8)
                r = lax.rsqrt(wide(cols[k][tk], sk))
                m = {t: cols[k][t] * r for t in range(tk, tiles)}
                m[tk] = jnp.where(sub8 > sk, m[tk], 0.0)
                for j in range(k + 1, SB):
                    c = wide(cols[j][tk], sk) * r
                    for t in range(tk, tiles):
                        cols[j][t] = cols[j][t] - m[t] * c
                for h in range(halves):
                    u = wide(w[tk][h], sk) * r
                    for t in range(tk, tiles):
                        w[t][h] = w[t][h] - m[t] * u
                    w[tk][h] = jnp.where(sub8 == sk, u, w[tk][h])
        done = jnp.concatenate([jnp.concatenate(r, axis=1) for r in w], axis=0)
        placed = pltpu.roll(done, p * PB, 1)
        out_ref[pl.ds(pl.multiple_of(p * PB, PB), PB), :] = jnp.where(
            lane < (p + 1) * PB, placed, 0.0
        )

        @pl.when(p < n // PB - 1)
        def _():
            turned = pltpu.roll(done, n - PB, 1)
            rest = pltpu.roll(jnp.where(lane_rest < PB, 0.0, a_ref[PB:n, :]), n - PB, 1)
            high, middle, low = split(turned)
            step = lax.dot_general(
                jnp.concatenate([high, middle, low, high, middle, high], axis=0),
                jnp.concatenate([high, high, high, middle, middle, low], axis=0),
                (((0,), (0,)), ((), ())), preferred_element_type=F32,
            )
            a_ref[0 : n - PB, :] = rest - step[0 : n - PB]

        return carry

    lax.fori_loop(0, n // PB, panel, 0)


def kernel(
    vals_hbm, slot_hbm, omega_hbm, count_ref,
    basis_ref, proj_ref, core_ref,
    vals_ref, slot_ref, omega_ref,
    part, r1, relay, r2, own, s_all, pick, ready, a_all, meta,
    pair0, pair1, g_send, g_recv, z_near, z_far, g_all,
    gram, linv, factor, prod, strip, code1, unit1, code2, unit2, w1, c1, w2, c2,
    beyond_sem, load_sem, send_sem, r1_sem, relay_sem, r2_sem, s_sem, sib_sem, a_sem, m_sem, pick_sem, ready_sem,
    pair_sem, g_sem, near_sem, far_sem, ag_sem, half_sem, w1_sem, c1_sem, w2_sem, c2_sem,
):
    row, col = lax.axis_index("row"), lax.axis_index("col")
    z, y = lax.div(row, NY), lax.rem(row, NY)
    x, k = lax.div(col, NK), lax.rem(col, NK)
    sib = 1 - k
    q = y * NX + x
    pending = []
    pairs = (pair0, pair1)

    def around(i, n):
        return lax.rem(i + n, n)

    def at(zz, yy, xx, kk):
        return (zz * NY + yy, xx * NK + kk)

    def plane(qq):
        return at(z, lax.div(qq, NX), lax.rem(qq, NX), k)

    to_sib = at(z, y, x, sib)

    def copy(src, dst, recv_sem, device):
        return pltpu.make_async_remote_copy(
            src_ref=src, dst_ref=dst, send_sem=send_sem, recv_sem=recv_sem,
            device_id=device, device_id_type=MESH,
        )

    def go(c):
        c.start()
        pending.append(c.wait_send)

    def flush():
        while pending:
            pending.pop(0)()

    moves = ((slot_hbm, slot_ref), (vals_hbm, vals_ref), (omega_hbm, omega_ref))
    loads = [pltpu.make_async_copy(a, b, load_sem.at[i]) for i, (a, b) in enumerate(moves)]
    for load in loads:
        load.start()

    barrier = pltpu.get_barrier_semaphore()

    def greet(device):
        pl.semaphore_signal(barrier, inc=1, device_id=device, device_id_type=MESH)

    reach = (3, -3, 2, -2, 1, -1)
    for j in reach:
        greet(at(around(z + j, NZ), y, x, k))
    for j in range(1, NQ):
        greet(plane(around(q + j, NQ)))
    greet(to_sib)

    for load in loads:
        load.wait()

    col_blocks = omega_ref.shape[0]
    slots = vals_ref.shape[0]
    row_of, column, live, prods = [], [], [], []
    for b in range(slots):
        slot = slot_ref[0, b]
        on = count_ref[0, 0] > b
        row_of.append(lax.div(slot, col_blocks))
        live.append(jnp.where(on, 1.0, 0.0).astype(F32))
        picked = omega_ref[pl.ds(lax.rem(slot, col_blocks), 1)].reshape(BS, RANK)
        prods.append(jnp.dot(vals_ref[b], picked, preferred_element_type=F32))
        column.append(jnp.where(on, lax.rem(slot, col_blocks), -1))

    def fill(kk, xx):
        total = None
        for b in range(slots):
            here = row_of[b] == xx * NK + kk
            term = prods[b] * (jnp.where(here, 1.0, 0.0).astype(F32) * live[b])
            total = term if total is None else total + term
        part[pl.ds(kk, 1), pl.ds(xx, 1)] = total[None, None]

    pl.semaphore_wait(barrier, NQ + len(reach))
    for j in (3, -3):
        to = at(around(z + j, NZ), y, x, k)
        pl.semaphore_signal(beyond_sem, inc=1, device_id=to, device_id_type=MESH)

    def sib_copy(xx):
        return copy(part.at[sib, xx], r1.at[xx], r1_sem.at[xx], to_sib)

    half = BS // 2
    sides = (1, -1)

    def rows_of(i):
        return pl.ds(i * half, half)

    def relay_copy(i):
        src = part.at[k, around(x + 2, NX), rows_of(i)]
        return copy(src, relay.at[i], relay_sem.at[i], at(z, y, around(x + sides[i], NX), k))

    def x_copy(i, r):
        xx = around(x + sides[i], NX)
        src = part.at[k, xx, rows_of(r)]
        return copy(src, r2.at[i, rows_of(r)], r2_sem.at[i, r], at(z, y, xx, k))

    def a_copies(d):
        to = at(z, around(y + d, NY), x, k)
        return (
            copy(a_all.at[y], a_all.at[y], a_sem.at[d - 1], to),
            copy(meta.at[y], meta.at[y], m_sem.at[d - 1], to),
        )

    def join(d):
        xx = around(x + d, NX)
        sib_copy(xx).wait_recv()
        part[pl.ds(k, 1), pl.ds(xx, 1)] = (
            part[pl.ds(k, 1), pl.ds(xx, 1)] + r1[pl.ds(xx, 1)][None]
        )

    for d in (2, 1, 3, 0):
        xx = around(x + d, NX)
        fill(sib, xx)
        go(sib_copy(xx))
    for xx in range(NX):
        fill(k, xx)
    for b in range(slots):
        a_all[pl.ds(y, 1), b] = (vals_ref[b] * live[b].astype(jnp.bfloat16))[None]
        meta[pl.ds(y, 1), b] = jnp.full((1,) + meta.shape[2:], column[b], jnp.int32)
    join(2)
    for i in range(2):
        go(relay_copy(i))
    for i in range(2):
        join(sides[i])
        go(x_copy(i, 1 - i))
    join(0)
    for i in range(2):
        relay_copy(i).wait_recv()
        at_rows = (pl.ds(k, 1), pl.ds(around(x + sides[i], NX), 1), rows_of(i))
        part[at_rows] = part[at_rows] + relay[i][None, None]
        go(x_copy(i, i))
    for i in range(2):
        for r in range(2):
            x_copy(i, r).wait_recv()
    own[...] = part[pl.ds(k, 1), pl.ds(x, 1)].reshape(BS, RANK) + r2[0] + r2[1]

    def gram_half(u, rows):
        pair = pairs[u]
        pair[pl.ds(k, 1)] = rows[None]
        go(copy(pair.at[k], pair.at[k], pair_sem.at[u], to_sib))
        copy(pair.at[k], pair.at[sib], pair_sem.at[u], to_sib).wait_recv()
        n = NK * rows.shape[0]
        lanes = pl.ds(pl.multiple_of(k * HALF, HALF), HALF)
        high, middle, low = split(pair[:, :, lanes].reshape(n, HALF))
        left = jnp.concatenate([high, middle, low, high, middle, high], axis=0)
        high, middle, low = split(pair[...].reshape(n, RANK))
        right = jnp.concatenate([high, high, high, middle, middle, low], axis=0)
        term = lax.dot_general(
            left, right, (((0,), (0,)), ((), ())), preferred_element_type=F32
        )
        g_send[u] = term.reshape(NQ, PIECE, RANK)
        for j in range(1, NQ):
            qq = around(q + j, NQ)
            go(copy(g_send.at[u, qq], g_recv.at[u, q], g_sem.at[u], plane(qq)))
        g_recv[u, pl.ds(q, 1)] = g_send[u, pl.ds(q, 1)]

    def arrived(buffer, sem):
        copy(buffer, buffer, sem, to_sib).wait_recv()

    group, member = lax.div(z, NG), lax.rem(z, NG)
    way, reach0 = lax.div(member, 2) * 2 - 1, 4 - member * (3 - member)

    def reduce_plane(u):
        arrived(g_recv.at[u, pl.ds(0, NQ - 1)], g_sem.at[u])
        total = g_recv[u, 0]
        for i in range(1, NQ):
            total = total + g_recv[u, i]
        z_near[u, pl.ds(member, 1)] = total[None]
        mine = z_near.at[u, member]
        for j in range(1, NG):
            near = group * NG + around(member + j, NG)
            go(copy(mine, mine, near_sem.at[u], at(near, y, x, k)))

    def reduce_near(u):
        arrived(z_near.at[u, pl.ds(0, NG - 1)], near_sem.at[u])
        total = z_near[u, 0]
        for i in range(1, NG):
            total = total + z_near[u, i]
        z_far[u, pl.ds(group, 1)] = total[None]
        mine = z_far.at[u, group]
        if u == 0:
            pl.semaphore_wait(beyond_sem, 2)
        for j in (2, 1, 0):
            far = around(z + way * (reach0 + j), NZ)
            go(copy(mine, mine, far_sem.at[u], at(far, y, x, k)))

    def reduce_far(u):
        arrived(z_far.at[u, pl.ds(0, NZ // NG - 1)], far_sem.at[u])
        total = z_far[u, 0]
        for i in range(1, NZ // NG):
            total = total + z_far[u, i]
        total = total * (1.0 / (BS * RB * NY * NZ) if u == 0 else 1.0 / (col_blocks * BS * NX * NK))
        g_all[u, pl.ds(k, 1), pl.ds(q, 1)] = total[None, None]
        mine = g_all.at[u, k, q]
        for j in range(1, NQ):
            go(copy(mine, mine, ag_sem.at[u], plane(around(q + j, NQ))))

    def gather_plane(u):
        flush()
        arrived(g_all.at[u, k, pl.ds(0, NQ - 1)], ag_sem.at[u])
        go(copy(g_all.at[u, k], g_all.at[u, k], half_sem.at[u], to_sib))
        copy(g_all.at[u, k], g_all.at[u, sib], half_sem.at[u], to_sib).wait_recv()
        return g_all[u].reshape(RANK, RANK)

    gram_half(0, own[...])

    parts = 2
    depth = BS // parts

    def s_copy(d, i):
        rows = pl.ds(i * depth, depth)
        return copy(
            own.at[rows], s_all.at[k, x, rows], s_sem.at[d - 1, i], at(z, y, around(x + d, NX), k)
        )

    def s_arrival(d, i):
        rows = pl.ds(i * depth, depth)
        return copy(
            own.at[rows], s_all.at[k, around(x - d, NX), rows], s_sem.at[d - 1, i], to_sib
        )

    def pick_copy(d):
        return copy(pick.at[y], pick.at[y], pick_sem.at[d - 1], at(z, around(y + d, NY), x, k))

    def pick_arrival(d):
        yy = around(y - d, NY)
        return copy(pick.at[y], pick.at[yy], pick_sem.at[d - 1], at(z, yy, x, k))

    s_all[pl.ds(k, 1), pl.ds(x, 1)] = own[...][None, None]
    reduce_plane(0)
    for d in (2, 1, 3):
        go(s_copy(d, 0))
    reduce_near(0)
    for d in (2, 1, 3):
        go(s_copy(d, 1))
    for d in (2, 1, 3):
        for c in a_copies(d):
            go(c)
    reduce_far(0)
    for d in (1, 3, 2):
        for i in range(parts):
            s_arrival(d, i).wait_recv()
    go(copy(s_all.at[k], s_all.at[k], sib_sem, to_sib))
    copy(s_all.at[k], s_all.at[sib], sib_sem, to_sib).wait_recv()
    for b in range(slots):
        rows = s_all[pl.ds(lax.rem(row_of[b], NK), 1), pl.ds(lax.div(row_of[b], NK), 1)]
        pick[pl.ds(y, 1), b] = rows.reshape(1, BS, RANK)
    gram[...] = gather_plane(0)

    for d in (1, 3):
        go(pick_copy(d))
    inverse_factor(gram, linv)

    high, middle, low = split(linv[...].T)
    for i, v in enumerate((high, high, high, middle, middle, low)):
        factor[pl.ds(i * RANK, RANK), :] = v

    def basis_rows(rows):
        high, middle, low = split(rows)
        wide = jnp.concatenate([high, middle, low, high, middle, high], axis=1)
        return jnp.dot(wide, factor[...], preferred_element_type=F32).astype(jnp.bfloat16)

    before, after, across = around(y - 1, NY), around(y + 1, NY), around(y + 2, NY)
    part0, part1 = pl.ds(0, slots // 2), pl.ds(slots // 2, slots - slots // 2)

    def pass_on(i, yy):
        blocks = (part0, part1)[i]
        to = at(z, (after, before)[i], x, k)
        return copy(ready.at[yy, blocks], ready.at[yy, blocks], ready_sem.at[i], to)

    def form(*which):
        rows = basis_rows(
            jnp.concatenate([pick[pl.ds(yy, 1), b].reshape(b.size * BS, RANK) for yy, b in which])
        )
        at_row = 0
        for yy, b in which:
            ready[pl.ds(yy, 1), b] = rows[at_row : at_row + b.size * BS].reshape(
                1, b.size, BS, RANK
            )
            at_row += b.size * BS

    for d in (1, 3):
        pick_arrival(d).wait_recv()
    form((before, part0), (after, part1))
    go(pass_on(0, before))
    go(pass_on(1, after))
    form((y, pl.ds(0, slots)))
    form((before, part1), (after, part0))
    basis_ref[...] = basis_rows(own[...])

    def products(yy):
        def one(b, carry):
            prod[pl.ds(yy, 1), pl.ds(b, 1)] = lax.dot_general(
                a_all[pl.ds(yy, 1), pl.ds(b, 1)].reshape(BS, BS),
                ready[pl.ds(yy, 1), pl.ds(b, 1)].reshape(BS, RANK),
                (((0,), (0,)), ((), ())), preferred_element_type=F32,
            )[None, None]
            return carry

        lax.fori_loop(0, slots, one, 0)

    products(y)
    for d in (1, 3, 2):
        yy = around(y - d, NY)
        to = at(z, yy, x, k)
        copy(a_all.at[y], a_all.at[yy], a_sem.at[d - 1], to).wait_recv()
        copy(meta.at[y], meta.at[yy], m_sem.at[d - 1], to).wait_recv()
        if d == 2:
            pass_on(0, across).wait_recv()
            pass_on(1, across).wait_recv()
        products(yy)

    tile = 16
    per_strip = STRIP // tile

    def coded(v):
        top = jnp.maximum(jnp.max(jnp.abs(v), axis=0, keepdims=True), 1e-33)
        return jnp.round(v * (STEPS / top)).astype(jnp.int32).astype(jnp.int16), top * (1.0 / STEPS)

    def value(steps, unit):
        return steps.astype(jnp.int32).astype(F32) * unit

    def place(zz, carry):
        totals = []
        for t in range(per_strip):
            g = zz * (NY * per_strip) + y * per_strip + t
            block = lax.div(g, BS // tile)
            rows = pl.multiple_of(lax.rem(g, BS // tile) * tile, tile)
            total = jnp.zeros((tile, RANK), F32)
            for yy in range(NY):
                for b in range(slots):
                    here = jnp.concatenate([meta[yy, b] == block] * (RANK // 128), axis=1)
                    total = total + jnp.where(here, prod[yy, b, pl.ds(rows, tile), :], 0.0)
            totals.append(total)
        total = jnp.concatenate(totals, axis=0)
        strip[pl.ds(zz, 1)] = total[None]
        steps, unit = coded(total)
        code1[pl.ds(zz, 1)] = steps[None]
        unit1[pl.ds(zz, 1)] = unit[None]
        return carry


    sign = 1 - 2 * k
    near = (1, -1, 2)

    def w1_copy(i, e):
        mid = around(z + sign * near[i], NZ)
        dest = around(mid + FAR[e], NZ)
        return copy(code1.at[dest], w1.at[e, i], w1_sem.at[e, i], at(mid, y, x, k))

    def c1_copy(i, e):
        mid = around(z + sign * near[i], NZ)
        dest = around(mid + FAR[e], NZ)
        return copy(unit1.at[dest], c1.at[e, i], c1_sem.at[e, i], at(mid, y, x, k))

    def w2_copies(e):
        to = at(around(z + FAR[e], NZ), y, x, k)
        return (
            copy(code2.at[e], w2.at[e], w2_sem.at[e], to),
            copy(unit2.at[e], c2.at[e], c2_sem.at[e], to),
        )

    for e in range(4):

        def put(i, carry):
            step = jnp.where(i == 3, 0, jnp.where(i == 2, 2, 1 - 2 * i))
            return place(around(around(z + sign * step, NZ) + FAR[e], NZ), carry)

        lax.fori_loop(0, 4, put, 0)
        for i in (2, 0, 1):
            go(w1_copy(i, e))
            go(c1_copy(i, e))
    for e in range(4):
        dest = around(z + FAR[e], NZ)
        total = strip[pl.ds(dest, 1)].reshape(STRIP, RANK)
        for i in range(3):
            w1_copy(i, e).wait_recv()
            c1_copy(i, e).wait_recv()
            total = total + value(w1[e, i], c1[e, i])
        code2[e], unit2[e] = coded(total)
        for c in w2_copies(e):
            go(c)
    proj = jnp.zeros((STRIP, RANK), F32)
    for e in range(4):
        for c in w2_copies(e):
            c.wait_recv()
        proj = proj + value(w2[e], c2[e])
    proj = proj * (1.0 / 256.0)
    proj_ref[0] = proj

    gram_half(1, proj)
    reduce_plane(1)
    reduce_near(1)
    reduce_far(1)
    core_ref[...] = gather_plane(1)

    flush()


def body(block_vals, block_slot, block_count, omega):
    slots = block_vals.shape[0]
    vmem = pl.BlockSpec(memory_space=pltpu.VMEM)
    hbm = pl.BlockSpec(memory_space=pltpu.HBM)
    dma = pltpu.SemaphoreType.DMA
    blocks = lambda *lead: pltpu.VMEM((*lead, BS, RANK), F32)
    inputs = [
        pltpu.with_memory_space_constraint(a, pltpu.HBM)
        for a in (block_vals, block_slot.T, omega.reshape(-1, BS, RANK))
    ]
    basis, projected, core = pl.pallas_call(
        kernel,
        out_shape=(
            pltpu.VMEM((BS, RANK), jnp.bfloat16),
            pltpu.VMEM((1, STRIP, RANK), F32),
            pltpu.VMEM((RANK, RANK), F32),
        ),
        in_specs=[hbm] * 3 + [pl.BlockSpec(memory_space=pltpu.SMEM)],
        out_specs=(vmem, vmem, vmem),
        scratch_shapes=[
            pltpu.VMEM(block_vals.shape, block_vals.dtype),
            pltpu.SMEM(block_slot.shape[::-1], jnp.int32),
            pltpu.VMEM((omega.shape[0] // BS, BS, RANK), omega.dtype),
            blocks(NK, NX),
            blocks(NX),
            pltpu.VMEM((2, BS // 2, RANK), F32),
            blocks(2),
            blocks(),
            blocks(NK, NX),
            blocks(NY, slots),
            pltpu.VMEM((NY, slots, BS, RANK), jnp.bfloat16),
            pltpu.VMEM((NY, slots, BS, BS), jnp.bfloat16),
            pltpu.VMEM((NY, slots, 16, 128), jnp.int32),
            blocks(NK),
            pltpu.VMEM((NK, STRIP, RANK), F32),
            pltpu.VMEM((2, NQ, PIECE, RANK), F32),
            pltpu.VMEM((2, NQ, PIECE, RANK), F32),
            pltpu.VMEM((2, NG, PIECE, RANK), F32),
            pltpu.VMEM((2, NZ // NG, PIECE, RANK), F32),
            pltpu.VMEM((2, NK, NQ, PIECE, RANK), F32),
            pltpu.VMEM((RANK, RANK), F32),
            pltpu.VMEM((RANK, RANK), F32),
            pltpu.VMEM((6 * RANK, RANK), jnp.bfloat16),
            blocks(NY, slots),
            pltpu.VMEM((NZ, STRIP, RANK), F32),
            pltpu.VMEM((NZ, STRIP, RANK), jnp.int16),
            pltpu.VMEM((NZ, 1, RANK), F32),
            pltpu.VMEM((4, STRIP, RANK), jnp.int16),
            pltpu.VMEM((4, 1, RANK), F32),
            pltpu.VMEM((4, 3, STRIP, RANK), jnp.int16),
            pltpu.VMEM((4, 3, 1, RANK), F32),
            pltpu.VMEM((4, STRIP, RANK), jnp.int16),
            pltpu.VMEM((4, 1, RANK), F32),
            pltpu.SemaphoreType.REGULAR,
            dma((3,)), dma,
            dma((NX,)), dma((2,)), dma((2, 2)), dma((NX - 1, 2)), dma, dma((NY - 1,)), dma((NY - 1,)), dma((NY - 1,)), dma((2,)),
            dma((2,)), dma((2,)), dma((2,)), dma((2,)), dma((2,)), dma((2,)), dma((4, 3)), dma((4, 3)), dma((4,)), dma((4,)),
        ],
        compiler_params=pltpu.CompilerParams(
            collective_id=0, has_side_effects=True, vmem_limit_bytes=60 * 2**20
        ),
        name="range_basis",
    )(*inputs, block_count)
    return basis, projected, core


def solution(mesh):
    placed = (P("row", "col", None), P("row", "col"), P("row", "col"), P("col", None))
    return jax.shard_map(
        body,
        mesh=mesh,
        in_specs=placed,
        out_specs=(P(("row", "col"), None), P("col", "row", None), P()),
        check_vma=False,
    )
```
